32 devices in a mesh: grp: 2 (over core), exp: 16 (over z, y, x).
Axes of the slice: x: 2, y: 2, z: 4, core: 2. Of those that a mesh axis runs over, the one named last changes fastest.
Arguments:
- tokens: bfloat16 [4096, 7168], P('exp', 'grp'), may hold values from -6 to 6
- d_out: bfloat16 [4096, 7168], P('exp', 'grp'), may hold values from -6 to 6
- row_expert: int32 [4096], P('exp'), may hold values from 0 to 15, as said below
- w_gate_up: bfloat16 [16, 7168, 2, 1024], P('exp', 'grp'), may hold values from -0.0625 to 0.0625
- w_down: bfloat16 [16, 1024, 7168], P('exp', None, 'grp'), may hold values from -0.1875 to 0.1875
Outputs:
- token_grads: bfloat16 [4096, 7168], P('exp', 'grp')
- gate_up_grads: bfloat16 [16, 7168, 2, 1024], P('exp', 'grp')
- down_grads: bfloat16 [16, 1024, 7168], P('exp', None, 'grp')
The draws below stay inside these ranges and needn't reach their ends.
Inputs may be any that keep to these rules, and one draw needn't show every extreme that they name: `row_expert`: in each block of 256 rows held by one index of exp, one expert, the same for every block, is named by exactly 64 rows; every other expert by at most 32 rows, and in every block some expert by exactly 32.
All inputs are finite; a program needn't handle non-finite values.
Results may differ from the reference program's by a relative error of at most 0.028.
Values may be sent and summed in bfloat16 or wider, within the bound.
No kernel may reach another device: no remote copies, remote signals or barrier semaphores. Data moves between devices by JAX's collectives and lax.ppermute only.
A program may use at most 192 MiB of HBM per device.

```python
import jax
import jax.numpy as jnp
from jax import lax

D = 7168
HIDDEN_SIZE = 1024
ROWS_DEV = 256
EXPERTS = 16
TOKENS = 4096
CAP = 32
HOT_CAP = 64
N_GRP = 2
N_EXP = 16


def draw_row_expert(key, part):
    key = jax.random.fold_in(key, 11)
    hot_key, block_key = jax.random.split(key)
    hot_expert = jax.random.randint(hot_key, (), 0, N_EXP)
    cold_cap = 2 * ROWS_DEV // N_EXP
    hot_cap = 4 * ROWS_DEV // N_EXP
    cold_rows = ROWS_DEV - hot_cap
    slot_total = (N_EXP - 1) * cold_cap

    def one_block(block_number):
        one_key = jax.random.fold_in(block_key, block_number)
        first_key, second_key, third_key = jax.random.split(one_key, 3)
        full_cold = jax.random.randint(first_key, (), 0, N_EXP - 1)
        slot_owner = jnp.arange(slot_total, dtype=jnp.int32) // cold_cap
        random_part = jax.random.randint(second_key, (slot_total,), 0, 1 << 16)
        positions = jnp.arange(slot_total, dtype=jnp.int32)
        sort_score = random_part * slot_total + positions
        sort_score = jnp.where(slot_owner == full_cold, positions - slot_total, sort_score)
        slot_order = jnp.argsort(sort_score)
        chosen = slot_owner[slot_order[:cold_rows]]
        chosen = jnp.where(chosen >= hot_expert, chosen + 1, chosen)
        source_rows = jnp.concatenate([jnp.full((hot_cap,), hot_expert, dtype=jnp.int32), chosen.astype(jnp.int32)])
        return jax.random.permutation(third_key, source_rows)
    return jax.vmap(one_block)(jnp.arange(N_EXP)).reshape(-1).astype(jnp.int32)


def block_scale(key, extent, cuts, smallest, high):
    def one(position, parts):
        heights = jax.random.uniform(jax.random.fold_in(jax.random.fold_in(key, 6), position), (parts,), jnp.float32, smallest / len(cuts), high / len(cuts))
        return jnp.repeat(jnp.exp(heights), extent[position] // parts).reshape((-1,) + (1,) * (len(extent) - position - 1))

    level = one(*cuts[0])
    for cut in cuts[1:]:
        level = level * one(*cut)
    return level


def centred(stream_key, extent, scale, limit, cuts=(), kind=jnp.bfloat16):
    values = scale * jax.random.normal(stream_key, extent, jnp.float32)
    if cuts:
        values = values * block_scale(stream_key, extent, cuts, -0.22, 0.18)
    return jnp.clip(values, -limit, limit).astype(kind)


def setup_inputs(seed: int = 0) -> dict:
    splits = jax.random.split(jax.random.key(seed), 6)
    tokens = centred(splits[0], (TOKENS, D), 1.0, 6.0, ((0, 16), (1, 2)))
    d_out = centred(splits[1], (TOKENS, D), 1.0, 6.0, ((0, 16), (1, 2)))
    row_expert = draw_row_expert(jax.random.fold_in(splits[5], 71), 0)
    w_gate_up = centred(splits[3], (EXPERTS, D, 2, HIDDEN_SIZE), D ** -0.5, 0.0625, ((0, 16), (1, 2)))
    w_down = centred(splits[4], (EXPERTS, HIDDEN_SIZE, D), HIDDEN_SIZE ** -0.5, 0.1875, ((0, 16), (2, 2)))
    return dict(tokens=tokens, d_out=d_out, row_expert=row_expert, w_gate_up=w_gate_up, w_down=w_down)


def silu_parts(gate_value):
    sigmoid_value = jax.nn.sigmoid(gate_value)
    return gate_value * sigmoid_value, sigmoid_value * (1.0 + gate_value * (1.0 - sigmoid_value))


def blocked_product(left, right):
    block_rows = left.shape[0]
    feature_share = D // N_GRP
    left_blocks = left.reshape(block_rows, N_GRP, feature_share).astype(jnp.float32)
    right_blocks = right.reshape(N_GRP, feature_share, right.shape[1]).astype(jnp.float32)
    partials = jnp.einsum("bgk,gkn->gbn", left_blocks, right_blocks).astype(jnp.bfloat16)
    partials = lax.optimization_barrier(partials)
    return jnp.sum(partials.astype(jnp.float32), axis=0)


def expert_block(tokens, d_out, w_gate_up, w_down, row_order, start_row, row_total, expert, block_rows):
    row_index = lax.dynamic_slice_in_dim(row_order, start_row.astype(jnp.int32), block_rows)
    is_valid = (jnp.arange(block_rows, dtype=jnp.int32) < row_total)[:, None]
    block_tokens = jnp.where(is_valid, tokens[row_index], jnp.zeros((), tokens.dtype))
    block_grads = jnp.where(is_valid, d_out[row_index], jnp.zeros((), d_out.dtype))
    gate_up_matrix = w_gate_up[expert].reshape(D, 2 * HIDDEN_SIZE)
    down_matrix = w_down[expert]
    gate_up = blocked_product(block_tokens, gate_up_matrix)
    hidden_grads = blocked_product(block_grads, jnp.transpose(down_matrix))
    activated, gate_slope = silu_parts(gate_up[:, :HIDDEN_SIZE])
    upward = gate_up[:, HIDDEN_SIZE:]
    hidden = (activated * upward).astype(jnp.bfloat16)
    branch_grads = jnp.concatenate([hidden_grads * upward * gate_slope, hidden_grads * activated], axis=1).astype(jnp.bfloat16)
    down_grads = lax.dot_general(hidden, block_grads, (((0,), (0,)), ((), ())), preferred_element_type=jnp.float32).astype(jnp.bfloat16)
    gate_up_grads = lax.dot_general(block_tokens, branch_grads, (((0,), (0,)), ((), ())), preferred_element_type=jnp.float32).astype(jnp.bfloat16).reshape(D, 2, HIDDEN_SIZE)
    row_grads = lax.dot_general(branch_grads, gate_up_matrix, (((1,), (1,)), ((), ())), preferred_element_type=jnp.float32).astype(jnp.bfloat16)
    row_grads = jnp.where(is_valid, row_grads, jnp.zeros((), row_grads.dtype))
    return row_index, row_grads, gate_up_grads, down_grads


def reference(tokens, d_out, row_expert, w_gate_up, w_down):
    total = tokens.shape[0]
    expert_ids = jnp.arange(EXPERTS, dtype=jnp.int32)
    expert_loads = jnp.sum((row_expert[:, None] == expert_ids[None, :]).astype(jnp.int32), axis=0).astype(jnp.int32)
    expert_starts = (jnp.cumsum(expert_loads) - expert_loads).astype(jnp.int32)
    sort_keys = row_expert.astype(jnp.int32) * total + jnp.arange(total, dtype=jnp.int32)
    row_order = jnp.argsort(sort_keys).astype(jnp.int32)
    hot_block = N_EXP * HOT_CAP
    cold_block = N_EXP * CAP
    row_order = jnp.concatenate([row_order, jnp.zeros((hot_block,), jnp.int32)])
    hot_expert = jnp.argmax(expert_loads).astype(jnp.int32)

    def cold_step(token_grads, expert):
        row_total = jnp.where(expert == hot_expert, 0, expert_loads[expert]).astype(jnp.int32)
        row_index, row_grads, gate_up_grads, down_grads = expert_block(tokens, d_out, w_gate_up, w_down, row_order, expert_starts[expert], row_total, expert, cold_block)
        return token_grads.at[row_index].add(row_grads), (gate_up_grads, down_grads)

    token_grads, (gate_up_all, down_all) = lax.scan(cold_step, jnp.zeros_like(tokens), expert_ids)
    row_index, row_grads, hot_gate_up, hot_down = expert_block(tokens, d_out, w_gate_up, w_down, row_order, expert_starts[hot_expert], expert_loads[hot_expert], hot_expert, hot_block)
    token_grads = token_grads.at[row_index].add(row_grads)
    gate_up_all = gate_up_all.at[hot_expert].set(hot_gate_up)
    down_all = down_all.at[hot_expert].set(hot_down)
    return token_grads, gate_up_all, down_all
```

```python
import jax
import jax.numpy as jnp
from jax import lax
from jax.sharding import PartitionSpec as P


def rank_in_expert(row_expert):
    row_count = row_expert.shape[0]
    same = row_expert[:, None] == row_expert[None, :]
    earlier = jnp.arange(row_count)[None, :] < jnp.arange(row_count)[:, None]
    return jnp.sum((same & earlier).astype(jnp.int32), axis=1)


def one_hot(index, total):
    return (index[None, :] == jnp.arange(total, dtype=jnp.int32)[:, None]).astype(jnp.bfloat16)


def place(one_hot_rows, rows):
    return lax.dot_general(
        one_hot_rows, rows, (((1,), (0,)), ((), ())), preferred_element_type=jnp.float32
    ).astype(jnp.bfloat16)


def exchange(rows, expert_count):
    slots, width = rows.shape
    return lax.all_to_all(
        rows.reshape(expert_count, slots // expert_count, width),
        "exp",
        split_axis=0,
        concat_axis=0,
        tiled=True,
    ).reshape(slots, width)


def sum_over_grp(part):
    part = part.astype(jnp.bfloat16)
    if lax.axis_size("grp") == 2:
        other = lax.ppermute(part, "grp", [(0, 1), (1, 0)])
        return part.astype(jnp.float32) + other.astype(jnp.float32)
    return lax.psum(part, "grp").astype(jnp.float32)


def activate(gate_up, hidden_grads):
    hidden_width = hidden_grads.shape[1]
    gate_value = gate_up[:, :hidden_width]
    upward = gate_up[:, hidden_width:]
    sigmoid_value = jax.nn.sigmoid(gate_value)
    activated = gate_value * sigmoid_value
    gate_slope = sigmoid_value * (1.0 + gate_value * (1.0 - sigmoid_value))
    hidden = (activated * upward).astype(jnp.bfloat16)
    branch = jnp.concatenate(
        [hidden_grads * upward * gate_slope, hidden_grads * activated], axis=1
    ).astype(jnp.bfloat16)
    return hidden, branch


def forward(rows_in, grads_in, gate_up_matrix, down_matrix):
    gate_up = sum_over_grp(jnp.dot(rows_in, gate_up_matrix, preferred_element_type=jnp.float32))
    hidden_grads = sum_over_grp(
        lax.dot_general(
            grads_in, down_matrix, (((1,), (1,)), ((), ())), preferred_element_type=jnp.float32
        )
    )
    return activate(gate_up, hidden_grads)


def row_gradients(branch, gate_up_matrix):
    return lax.dot_general(
        branch, gate_up_matrix, (((1,), (1,)), ((), ())), preferred_element_type=jnp.float32
    ).astype(jnp.bfloat16)


def outer(left, right):
    return lax.dot_general(
        left, right, (((0,), (0,)), ((), ())), preferred_element_type=jnp.float32
    ).astype(jnp.bfloat16)


def local(tokens, d_out, row_expert, w_gate_up, w_down):
    row_count, feature_share = tokens.shape
    hidden_width = w_down.shape[1]
    expert_count = lax.axis_size("exp")
    gate_up_matrix = w_gate_up.reshape(feature_share, 2 * hidden_width)
    down_matrix = w_down.reshape(hidden_width, feature_share)
    cap = 2 * row_count // expert_count
    half = cap // 2

    rank = rank_in_expert(row_expert)
    is_spill = rank >= cap
    busiest = jnp.max(jnp.where(is_spill, row_expert, -1))
    is_busiest = lax.axis_index("exp") == busiest
    spill_hot = one_hot(jnp.where(is_spill, rank - cap, -1), cap)
    chunk_hot = []
    for chunk in range(2):
        inside = (rank >= chunk * half) & (rank < (chunk + 1) * half)
        slot = row_expert * half + rank - chunk * half
        chunk_hot.append(one_hot(jnp.where(inside, slot, -1), expert_count * half))

    spill_rows = lax.all_gather(place(spill_hot, tokens), "exp", tiled=True)
    spill_grads = lax.all_gather(place(spill_hot, d_out), "exp", tiled=True)
    chunk_rows = []
    chunk_grads = []
    for hot in chunk_hot:
        chunk_rows.append(exchange(place(hot, tokens), expert_count))
        chunk_grads.append(exchange(place(hot, d_out), expert_count))

    hidden, branch = forward(spill_rows, spill_grads, gate_up_matrix, down_matrix)
    hidden = jnp.where(is_busiest, hidden, jnp.zeros_like(hidden))
    branch = jnp.where(is_busiest, branch, jnp.zeros_like(branch))
    spill_back = lax.psum_scatter(
        row_gradients(branch, gate_up_matrix), "exp", scatter_dimension=0, tiled=True
    )
    all_hidden = [hidden]
    all_branch = [branch]
    back = []
    for rows_in, grads_in in zip(chunk_rows, chunk_grads):
        hidden, branch = forward(rows_in, grads_in, gate_up_matrix, down_matrix)
        all_hidden.append(hidden)
        all_branch.append(branch)
        back.append(exchange(row_gradients(branch, gate_up_matrix), expert_count))

    all_rows = jnp.concatenate([spill_rows] + chunk_rows, axis=0)
    all_grads = jnp.concatenate([spill_grads] + chunk_grads, axis=0)
    hidden = jnp.concatenate(all_hidden, axis=0)
    branch = jnp.concatenate(all_branch, axis=0)
    gate_up_grads = outer(all_rows, branch).reshape(1, feature_share, 2, hidden_width)
    down_grads = outer(hidden, all_grads).reshape(1, hidden_width, feature_share)

    pick = jnp.concatenate([spill_hot] + chunk_hot, axis=0)
    returned = jnp.concatenate([spill_back] + back, axis=0)
    token_grads = lax.dot_general(
        pick, returned, (((0,), (0,)), ((), ())), preferred_element_type=jnp.float32
    ).astype(jnp.bfloat16)
    return (token_grads, gate_up_grads, down_grads)


def solution(mesh):
    return jax.shard_map(
        local,
        mesh=mesh,
        in_specs=(
            P("exp", "grp"),
            P("exp", "grp"),
            P("exp"),
            P("exp", "grp", None, None),
            P("exp", None, "grp"),
        ),
        out_specs=(P("exp", "grp"), P("exp", "grp", None, None), P("exp", None, "grp")),
        check_vma=False,
    )
```

```python
import jax
import jax.numpy as jnp
from jax import lax
from jax.experimental.layout import Layout, with_layout_constraint
from jax.sharding import PartitionSpec as P


def rank_in_expert(row_expert):
    row_count = row_expert.shape[0]
    same = row_expert[:, None] == row_expert[None, :]
    earlier = jnp.arange(row_count)[None, :] < jnp.arange(row_count)[:, None]
    return jnp.sum((same & earlier).astype(jnp.int32), axis=1)


def one_hot(index, total):
    return (index[None, :] == jnp.arange(total, dtype=jnp.int32)[:, None]).astype(jnp.bfloat16)


def place(one_hot_rows, rows):
    return lax.dot_general(
        one_hot_rows, rows, (((1,), (0,)), ((), ())), preferred_element_type=jnp.float32
    ).astype(jnp.bfloat16)


def exchange(rows, expert_count):
    slots, width = rows.shape
    return lax.all_to_all(
        rows.reshape(expert_count, slots // expert_count, width),
        "exp",
        split_axis=0,
        concat_axis=0,
        tiled=True,
    ).reshape(slots, width)


def butterfly_masks(axis_total, swap):
    masks = []
    bit = axis_total // 2
    while bit:
        masks.append(bit)
        bit //= 2
    return masks[:-2] + masks[:-3:-1] if swap else masks


def swap_with(rows, mask):
    total = lax.axis_size("exp")
    return lax.ppermute(rows, "exp", [(i, i ^ mask) for i in range(total)])


def swap_quarters(rows):
    quarter = rows.shape[0] // 4
    parts = [rows[i * quarter : (i + 1) * quarter] for i in (0, 2, 1, 3)]
    return jnp.concatenate(parts, axis=0)


def spread(rows, swap):
    for mask in butterfly_masks(lax.axis_size("exp"), swap):
        rows = jnp.concatenate([rows, swap_with(rows, mask)], axis=0)
    return swap_quarters(rows) if swap else rows


def collect(rows, swap):
    if swap:
        rows = swap_quarters(rows)
    for mask in reversed(butterfly_masks(lax.axis_size("exp"), swap)):
        half = rows.shape[0] // 2
        rows = rows[:half] + swap_with(rows[half:], mask)
    return rows


def sum_over_grp(part):
    part = part.astype(jnp.bfloat16)
    if lax.axis_size("grp") == 2:
        other = lax.ppermute(part, "grp", [(0, 1), (1, 0)])
        return part.astype(jnp.float32) + other.astype(jnp.float32)
    return lax.psum(part, "grp").astype(jnp.float32)


def activate(gate_up, hidden_grads):
    hidden_width = hidden_grads.shape[1]
    gate_value = gate_up[:, :hidden_width]
    upward = gate_up[:, hidden_width:]
    sigmoid_value = jax.nn.sigmoid(gate_value)
    activated = gate_value * sigmoid_value
    gate_slope = sigmoid_value * (1.0 + gate_value * (1.0 - sigmoid_value))
    hidden = (activated * upward).astype(jnp.bfloat16)
    branch = jnp.concatenate(
        [hidden_grads * upward * gate_slope, hidden_grads * activated], axis=1
    ).astype(jnp.bfloat16)
    return hidden, branch


def forward(rows_in, grads_in, gate_up_matrix, down_matrix):
    gate_up = sum_over_grp(jnp.dot(rows_in, gate_up_matrix, preferred_element_type=jnp.float32))
    hidden_grads = sum_over_grp(
        lax.dot_general(
            grads_in, down_matrix, (((1,), (1,)), ((), ())), preferred_element_type=jnp.float32
        )
    )
    return activate(gate_up, hidden_grads)


def row_gradients(branch, gate_up_matrix):
    return lax.dot_general(
        branch, gate_up_matrix, (((1,), (1,)), ((), ())), preferred_element_type=jnp.float32
    ).astype(jnp.bfloat16)


def outer(left, right):
    return lax.dot_general(
        left, right, (((0,), (0,)), ((), ())), preferred_element_type=jnp.float32
    ).astype(jnp.bfloat16)


def local(tokens, d_out, row_expert, w_gate_up, w_down):
    row_count, feature_share = tokens.shape
    hidden_width = w_down.shape[1]
    expert_count = lax.axis_size("exp")
    gate_up_matrix = w_gate_up.reshape(feature_share, 2 * hidden_width)
    down_matrix = w_down.reshape(hidden_width, feature_share)
    cap = 2 * row_count // expert_count
    half = cap // 2

    rank = rank_in_expert(row_expert)
    is_spill = rank >= cap
    busiest = jnp.max(jnp.where(is_spill, row_expert, -1))
    is_busiest = lax.axis_index("exp") == busiest
    spill_hot = one_hot(jnp.where(is_spill, rank - cap, -1), cap)
    chunk_hot = []
    for chunk in range(2):
        inside = (rank >= chunk * half) & (rank < (chunk + 1) * half)
        slot = row_expert * half + rank - chunk * half
        chunk_hot.append(one_hot(jnp.where(inside, slot, -1), expert_count * half))

    both = jnp.concatenate([tokens, d_out], axis=1)
    arrived = [exchange(place(hot, both), expert_count) for hot in chunk_hot]
    spill_rows = spread(place(spill_hot, tokens), False)
    spill_grads = spread(place(spill_hot, d_out), True)

    def chunk_step(both_in):
        rows_in, grads_in = both_in[:, :feature_share], both_in[:, feature_share:]
        hidden, branch = forward(rows_in, grads_in, gate_up_matrix, down_matrix)
        return rows_in, grads_in, hidden, branch, row_gradients(branch, gate_up_matrix)

    rows_0, grads_0, hidden_0, branch_0, out_0 = chunk_step(arrived[0])
    hidden_s, branch_s = forward(spill_rows, spill_grads, gate_up_matrix, down_matrix)
    hidden_s = jnp.where(is_busiest, hidden_s, jnp.zeros_like(hidden_s))
    branch_s = jnp.where(is_busiest, branch_s, jnp.zeros_like(branch_s))
    out_s = row_gradients(branch_s, gate_up_matrix)
    last_in, out_0, out_s = lax.optimization_barrier((arrived[1], out_0, out_s))
    rows_1, grads_1, hidden_1, branch_1, out_1 = chunk_step(last_in)
    split = feature_share // 2
    back_s = jnp.concatenate(
        [collect(out_s[:, :split], False), collect(out_s[:, split:], True)], axis=1
    )
    back_0 = exchange(out_0, expert_count)
    back_1 = exchange(out_1, expert_count)

    all_rows = jnp.concatenate([spill_rows, rows_0, rows_1], axis=0)
    all_grads = jnp.concatenate([spill_grads, grads_0, grads_1], axis=0)
    hidden = jnp.concatenate([hidden_s, hidden_0, hidden_1], axis=0)
    branch = jnp.concatenate([branch_s, branch_0, branch_1], axis=0)
    gate_up_grads = with_layout_constraint(outer(all_rows, branch), Layout((0, 1)))
    gate_up_grads = gate_up_grads.reshape(1, feature_share, 2, hidden_width)
    down_grads = outer(hidden, all_grads).reshape(1, hidden_width, feature_share)

    pick = jnp.concatenate([spill_hot] + chunk_hot, axis=0)
    returned = jnp.concatenate([back_s, back_0, back_1], axis=0)
    token_grads = lax.dot_general(
        pick, returned, (((0,), (0,)), ((), ())), preferred_element_type=jnp.float32
    ).astype(jnp.bfloat16)
    return (token_grads, gate_up_grads, down_grads)


def solution(mesh):
    return jax.shard_map(
        local,
        mesh=mesh,
        in_specs=(
            P("exp", "grp"),
            P("exp", "grp"),
            P("exp"),
            P("exp", "grp", None, None),
            P("exp", None, "grp"),
        ),
        out_specs=(P("exp", "grp"), P("exp", "grp", None, None), P("exp", None, "grp")),
        check_vma=False,
    )
```

```python
import jax
import jax.numpy as jnp
from jax import lax
from jax.experimental.layout import Layout, with_layout_constraint
from jax.sharding import PartitionSpec as P


def rank_in_expert(row_expert):
    row_count = row_expert.shape[0]
    same = row_expert[:, None] == row_expert[None, :]
    earlier = jnp.arange(row_count)[None, :] < jnp.arange(row_count)[:, None]
    return jnp.sum((same & earlier).astype(jnp.int32), axis=1)


def one_hot(index, total):
    return (index[None, :] == jnp.arange(total, dtype=jnp.int32)[:, None]).astype(jnp.bfloat16)


def place(one_hot_rows, rows):
    return lax.dot_general(
        one_hot_rows, rows, (((1,), (0,)), ((), ())), preferred_element_type=jnp.float32
    ).astype(jnp.bfloat16)


def exchange(rows, expert_count):
    slots, width = rows.shape
    return lax.all_to_all(
        rows.reshape(expert_count, slots // expert_count, width),
        "exp",
        split_axis=0,
        concat_axis=0,
        tiled=True,
    ).reshape(slots, width)


def swap_with(rows, mask):
    total = lax.axis_size("exp")
    return lax.ppermute(rows, "exp", [(i, i ^ mask) for i in range(total)])


def by_distance(blocks):
    total = lax.axis_size("exp")
    order = lax.axis_index("exp") ^ jnp.arange(total, dtype=jnp.int32)
    return jnp.concatenate(
        [lax.dynamic_slice_in_dim(blocks, order[k], 1, axis=0) for k in range(total)], axis=0
    )


def collect(blocks):
    half = lax.axis_size("exp") // 2
    pairs = [jnp.concatenate([blocks[k], blocks[k + half]], axis=0) for k in range(half)]
    arrived = [swap_with(pairs[k], k) for k in range(1, half)]
    total = pairs[0]
    for pair in arrived:
        total = total + pair
    height = blocks.shape[1]
    return total[:height] + swap_with(total[height:], half)


def sum_over_grp(part):
    part = part.astype(jnp.bfloat16)
    if lax.axis_size("grp") == 2:
        other = lax.ppermute(part, "grp", [(0, 1), (1, 0)])
        return part.astype(jnp.float32) + other.astype(jnp.float32)
    return lax.psum(part, "grp").astype(jnp.float32)


def activate(gate_up, hidden_grads):
    hidden_width = hidden_grads.shape[1]
    gate_value = gate_up[:, :hidden_width]
    upward = gate_up[:, hidden_width:]
    sigmoid_value = jax.nn.sigmoid(gate_value)
    activated = gate_value * sigmoid_value
    gate_slope = sigmoid_value * (1.0 + gate_value * (1.0 - sigmoid_value))
    hidden = (activated * upward).astype(jnp.bfloat16)
    branch = jnp.concatenate(
        [hidden_grads * upward * gate_slope, hidden_grads * activated], axis=1
    ).astype(jnp.bfloat16)
    return hidden, branch


def row_gradients(branch, gate_up_matrix):
    return lax.dot_general(
        branch, gate_up_matrix, (((1,), (1,)), ((), ())), preferred_element_type=jnp.float32
    ).astype(jnp.bfloat16)


def outer(left, right):
    return lax.dot_general(
        left, right, (((0,), (0,)), ((), ())), preferred_element_type=jnp.float32
    ).astype(jnp.bfloat16)


def local(tokens, d_out, row_expert, w_gate_up, w_down):
    row_count, feature_share = tokens.shape
    hidden_width = w_down.shape[1]
    expert_count = lax.axis_size("exp")
    gate_up_matrix = w_gate_up.reshape(feature_share, 2 * hidden_width)
    down_matrix = w_down.reshape(hidden_width, feature_share)
    cap = 2 * row_count // expert_count
    half = cap // 2

    rank = rank_in_expert(row_expert)
    is_spill = rank >= cap
    busiest = jnp.max(jnp.where(is_spill, row_expert, -1))
    is_busiest = lax.axis_index("exp") == busiest
    spill_hot = one_hot(jnp.where(is_spill, rank - cap, -1), cap)
    chunk_hot = []
    for chunk in range(2):
        inside = (rank >= chunk * half) & (rank < (chunk + 1) * half)
        slot = row_expert * half + rank - chunk * half
        chunk_hot.append(one_hot(jnp.where(inside, slot, -1), expert_count * half))

    both = jnp.concatenate([tokens, d_out], axis=1)

    def split(both_in):
        return both_in[:, :feature_share], both_in[:, feature_share:]

    def gate_up_of(rows_in, matrix):
        return sum_over_grp(jnp.dot(rows_in, matrix, preferred_element_type=jnp.float32))

    def hidden_grads_of(grads_in, matrix):
        return sum_over_grp(
            lax.dot_general(
                grads_in, matrix, (((1,), (1,)), ((), ())), preferred_element_type=jnp.float32
            )
        )

    arrived_0 = exchange(place(chunk_hot[0], both), expert_count)
    spill_rows = lax.all_gather(place(spill_hot, tokens), "exp", tiled=True)
    sent_1 = place(chunk_hot[1], both)
    sent_grads = place(spill_hot, d_out)
    arrived_0, spill_rows, sent_1, sent_grads, gate_up_matrix = lax.optimization_barrier(
        (arrived_0, spill_rows, sent_1, sent_grads, gate_up_matrix)
    )

    arrived_1 = exchange(sent_1, expert_count)
    spill_grads = lax.all_gather(sent_grads, "exp", tiled=True)
    rows_0, grads_0 = split(arrived_0)
    hidden_0, branch_0 = activate(
        gate_up_of(rows_0, gate_up_matrix), hidden_grads_of(grads_0, down_matrix)
    )
    out_0 = row_gradients(branch_0, gate_up_matrix)
    gate_up_s = gate_up_of(spill_rows, gate_up_matrix)
    arrived_1, spill_grads, hidden_0, branch_0, out_0, gate_up_s = lax.optimization_barrier(
        (arrived_1, spill_grads, hidden_0, branch_0, out_0, gate_up_s)
    )

    back_0 = exchange(out_0, expert_count)
    rows_1, grads_1 = split(arrived_1)
    hidden_1, branch_1 = activate(
        gate_up_of(rows_1, gate_up_matrix), hidden_grads_of(grads_1, down_matrix)
    )
    out_1 = row_gradients(branch_1, gate_up_matrix)
    hidden_s, branch_s = activate(gate_up_s, hidden_grads_of(spill_grads, down_matrix))
    hidden_s = jnp.where(is_busiest, hidden_s, jnp.zeros_like(hidden_s))
    branch_s = jnp.where(is_busiest, branch_s, jnp.zeros_like(branch_s))
    turned = by_distance(branch_s.reshape(expert_count, cap, -1)).reshape(branch_s.shape)
    out_s = row_gradients(turned, gate_up_matrix)
    back_0, out_1, out_s, hidden_1, branch_1, hidden_s, branch_s = lax.optimization_barrier(
        (back_0, out_1, out_s, hidden_1, branch_1, hidden_s, branch_s)
    )

    back_1 = exchange(out_1, expert_count)
    back_s = collect(out_s.reshape(expert_count, cap, feature_share))

    all_rows = jnp.concatenate([spill_rows, rows_0, rows_1], axis=0)
    all_grads = jnp.concatenate([spill_grads, grads_0, grads_1], axis=0)
    hidden = jnp.concatenate([hidden_s, hidden_0, hidden_1], axis=0)
    branch = jnp.concatenate([branch_s, branch_0, branch_1], axis=0)
    gate_up_grads = with_layout_constraint(outer(all_rows, branch), Layout((0, 1)))
    gate_up_grads = gate_up_grads.reshape(1, feature_share, 2, hidden_width)
    down_grads = outer(hidden, all_grads).reshape(1, hidden_width, feature_share)

    pick = jnp.concatenate([spill_hot] + chunk_hot, axis=0)
    returned = jnp.concatenate([back_s, back_0, back_1], axis=0)
    token_grads = lax.dot_general(
        pick, returned, (((0,), (0,)), ((), ())), preferred_element_type=jnp.float32
    ).astype(jnp.bfloat16)
    return (token_grads, gate_up_grads, down_grads)


def solution(mesh):
    return jax.shard_map(
        local,
        mesh=mesh,
        in_specs=(
            P("exp", "grp"),
            P("exp", "grp"),
            P("exp"),
            P("exp", "grp", None, None),
            P("exp", None, "grp"),
        ),
        out_specs=(P("exp", "grp"), P("exp", "grp", None, None), P("exp", None, "grp")),
        check_vma=False,
    )
```

```python
import jax
import jax.numpy as jnp
from jax import lax
from jax.experimental.layout import Layout, with_layout_constraint
from jax.sharding import PartitionSpec as P


def rank_in_expert(row_expert):
    row_count = row_expert.shape[0]
    same = row_expert[:, None] == row_expert[None, :]
    earlier = jnp.arange(row_count)[None, :] < jnp.arange(row_count)[:, None]
    return jnp.sum((same & earlier).astype(jnp.int32), axis=1)


def one_hot(index, total):
    return (index[None, :] == jnp.arange(total, dtype=jnp.int32)[:, None]).astype(jnp.bfloat16)


def place(one_hot_rows, rows):
    return lax.dot_general(
        one_hot_rows, rows, (((1,), (0,)), ((), ())), preferred_element_type=jnp.float32
    ).astype(jnp.bfloat16)


def exchange(rows, expert_count):
    slots, width = rows.shape
    return lax.all_to_all(
        rows.reshape(expert_count, slots // expert_count, width),
        "exp",
        split_axis=0,
        concat_axis=0,
        tiled=True,
    ).reshape(slots, width)


def swap_with(rows, mask):
    total = lax.axis_size("exp")
    return lax.ppermute(rows, "exp", [(i, i ^ mask) for i in range(total)])


def inner_masks(swap):
    masks = []
    bit = lax.axis_size("exp") // 4
    while bit:
        masks.append(bit)
        bit //= 2
    return masks[:-2] + masks[:-3:-1] if swap else masks


def swap_quarters(rows):
    quarter = rows.shape[0] // 4
    parts = [rows[i * quarter : (i + 1) * quarter] for i in (0, 2, 1, 3)]
    return jnp.concatenate(parts, axis=0)


def spread(rows, swap):
    for mask in inner_masks(swap):
        rows = jnp.concatenate([rows, swap_with(rows, mask)], axis=0)
    return swap_quarters(rows) if swap else rows


def collect(rows, swap):
    if swap:
        rows = swap_quarters(rows)
    for mask in reversed(inner_masks(swap)):
        half = rows.shape[0] // 2
        rows = rows[:half] + swap_with(rows[half:], mask)
    return rows


def sum_over_grp(part):
    part = part.astype(jnp.bfloat16)
    if lax.axis_size("grp") == 2:
        other = lax.ppermute(part, "grp", [(0, 1), (1, 0)])
        return part.astype(jnp.float32) + other.astype(jnp.float32)
    return lax.psum(part, "grp").astype(jnp.float32)


def activate(gate_up, hidden_grads):
    hidden_width = hidden_grads.shape[1]
    gate_value = gate_up[:, :hidden_width]
    upward = gate_up[:, hidden_width:]
    sigmoid_value = jax.nn.sigmoid(gate_value)
    activated = gate_value * sigmoid_value
    gate_slope = sigmoid_value * (1.0 + gate_value * (1.0 - sigmoid_value))
    hidden = (activated * upward).astype(jnp.bfloat16)
    branch = jnp.concatenate(
        [hidden_grads * upward * gate_slope, hidden_grads * activated], axis=1
    ).astype(jnp.bfloat16)
    return hidden, branch


def row_gradients(branch, gate_up_matrix):
    return lax.dot_general(
        branch, gate_up_matrix, (((1,), (1,)), ((), ())), preferred_element_type=jnp.float32
    ).astype(jnp.bfloat16)


def outer(left, right):
    return lax.dot_general(
        left, right, (((0,), (0,)), ((), ())), preferred_element_type=jnp.float32
    ).astype(jnp.bfloat16)


def local(tokens, d_out, row_expert, w_gate_up, w_down):
    row_count, feature_share = tokens.shape
    hidden_width = w_down.shape[1]
    expert_count = lax.axis_size("exp")
    gate_up_matrix = w_gate_up.reshape(feature_share, 2 * hidden_width)
    down_matrix = w_down.reshape(hidden_width, feature_share)
    cap = 2 * row_count // expert_count
    half = cap // 2

    rank = rank_in_expert(row_expert)
    is_spill = rank >= cap
    busiest = jnp.max(jnp.where(is_spill, row_expert, -1))
    is_busiest = lax.axis_index("exp") == busiest
    spill_hot = one_hot(jnp.where(is_spill, rank - cap, -1), cap)
    chunk_hot = []
    for chunk in range(2):
        inside = (rank >= chunk * half) & (rank < (chunk + 1) * half)
        slot = row_expert * half + rank - chunk * half
        chunk_hot.append(one_hot(jnp.where(inside, slot, -1), expert_count * half))

    both = jnp.concatenate([tokens, d_out], axis=1)

    def split(both_in):
        return both_in[:, :feature_share], both_in[:, feature_share:]

    def gate_up_of(rows_in, matrix):
        return sum_over_grp(jnp.dot(rows_in, matrix, preferred_element_type=jnp.float32))

    def hidden_grads_of(grads_in, matrix):
        return sum_over_grp(
            lax.dot_general(
                grads_in, matrix, (((1,), (1,)), ((), ())), preferred_element_type=jnp.float32
            )
        )

    far = expert_count // 2
    spill_both = place(spill_hot, both)
    spill_both = jnp.concatenate([spill_both, swap_with(spill_both, far)], axis=0)
    sent_0 = place(chunk_hot[0], both)
    spill_both, sent_0 = lax.optimization_barrier((spill_both, sent_0))

    arrived_0 = exchange(sent_0, expert_count)
    spill_rows, spill_grads = split(spill_both)
    spill_rows, spill_grads = spread(spill_rows, False), spread(spill_grads, True)
    sent_1 = place(chunk_hot[1], both)
    arrived_0, spill_rows, spill_grads, sent_1, gate_up_matrix = lax.optimization_barrier(
        (arrived_0, spill_rows, spill_grads, sent_1, gate_up_matrix)
    )

    arrived_1 = exchange(sent_1, expert_count)
    rows_0, grads_0 = split(arrived_0)
    hidden_0, branch_0 = activate(
        gate_up_of(rows_0, gate_up_matrix), hidden_grads_of(grads_0, down_matrix)
    )
    out_0 = row_gradients(branch_0, gate_up_matrix)
    hidden_s, branch_s = activate(
        gate_up_of(spill_rows, gate_up_matrix), hidden_grads_of(spill_grads, down_matrix)
    )
    hidden_s = jnp.where(is_busiest, hidden_s, jnp.zeros_like(hidden_s))
    branch_s = jnp.where(is_busiest, branch_s, jnp.zeros_like(branch_s))
    out_s = row_gradients(branch_s, gate_up_matrix)
    arrived_1, hidden_0, branch_0, out_0, hidden_s, branch_s, out_s = lax.optimization_barrier(
        (arrived_1, hidden_0, branch_0, out_0, hidden_s, branch_s, out_s)
    )

    back_0 = exchange(out_0, expert_count)
    middle = feature_share // 2
    back_s = jnp.concatenate(
        [collect(out_s[:, :middle], False), collect(out_s[:, middle:], True)], axis=1
    )
    rows_1, grads_1 = split(arrived_1)
    hidden_1, branch_1 = activate(
        gate_up_of(rows_1, gate_up_matrix), hidden_grads_of(grads_1, down_matrix)
    )
    out_1 = row_gradients(branch_1, gate_up_matrix)
    back_0, back_s, out_1, hidden_1, branch_1 = lax.optimization_barrier(
        (back_0, back_s, out_1, hidden_1, branch_1)
    )

    back_s = back_s[:cap] + swap_with(back_s[cap:], far)
    back_1 = exchange(out_1, expert_count)

    all_rows = jnp.concatenate([spill_rows, rows_0, rows_1], axis=0)
    all_grads = jnp.concatenate([spill_grads, grads_0, grads_1], axis=0)
    hidden = jnp.concatenate([hidden_s, hidden_0, hidden_1], axis=0)
    branch = jnp.concatenate([branch_s, branch_0, branch_1], axis=0)
    gate_up_grads = with_layout_constraint(outer(all_rows, branch), Layout((0, 1)))
    gate_up_grads = gate_up_grads.reshape(1, feature_share, 2, hidden_width)
    down_grads = outer(hidden, all_grads).reshape(1, hidden_width, feature_share)

    pick = jnp.concatenate([spill_hot] + chunk_hot, axis=0)
    returned = jnp.concatenate([back_s, back_0, back_1], axis=0)
    token_grads = lax.dot_general(
        pick, returned, (((0,), (0,)), ((), ())), preferred_element_type=jnp.float32
    ).astype(jnp.bfloat16)
    return (token_grads, gate_up_grads, down_grads)


def solution(mesh):
    return jax.shard_map(
        local,
        mesh=mesh,
        in_specs=(
            P("exp", "grp"),
            P("exp", "grp"),
            P("exp"),
            P("exp", "grp", None, None),
            P("exp", None, "grp"),
        ),
        out_specs=(P("exp", "grp"), P("exp", "grp", None, None), P("exp", None, "grp")),
        check_vma=False,
    )
```

```python
import functools

import jax
import jax.numpy as jnp
from jax import lax
from jax.experimental import pallas as pl
from jax.experimental.layout import Layout, with_layout_constraint
from jax.experimental.pallas import tpu as pltpu
from jax.sharding import PartitionSpec as P

VMEM_BYTES = 48 * 1024 * 1024


def rank_in_expert(row_expert):
    row_count = row_expert.shape[0]
    same = row_expert[:, None] == row_expert[None, :]
    earlier = jnp.arange(row_count)[None, :] < jnp.arange(row_count)[:, None]
    return jnp.sum((same & earlier).astype(jnp.int32), axis=1)


def one_hot(index, total):
    return (index[None, :] == jnp.arange(total, dtype=jnp.int32)[:, None]).astype(jnp.bfloat16)


def place(one_hot_rows, rows):
    return lax.dot_general(
        one_hot_rows, rows, (((1,), (0,)), ((), ())), preferred_element_type=jnp.float32
    ).astype(jnp.bfloat16)


def exchange(rows, expert_count):
    slots, width = rows.shape
    return lax.all_to_all(
        rows.reshape(expert_count, slots // expert_count, width),
        "exp",
        split_axis=0,
        concat_axis=0,
        tiled=True,
    ).reshape(slots, width)


def swap_with(rows, mask):
    total = lax.axis_size("exp")
    return lax.ppermute(rows, "exp", [(i, i ^ mask) for i in range(total)])


def double(rows, mask):
    return jnp.concatenate([rows, swap_with(rows, mask)], axis=0)


def halve(rows, mask):
    half = rows.shape[0] // 2
    return rows[:half] + swap_with(rows[half:], mask)


def outer_masks():
    masks = []
    bit = lax.axis_size("exp") // 2
    while bit > 2:
        masks.append(bit)
        bit //= 2
    return masks


def swap_quarters(rows):
    quarter = rows.shape[0] // 4
    parts = [rows[i * quarter : (i + 1) * quarter] for i in (0, 2, 1, 3)]
    return jnp.concatenate(parts, axis=0)


def spread(rows, swap):
    for mask in (1, 2) if swap else (2, 1):
        rows = double(rows, mask)
    return swap_quarters(rows) if swap else rows


def collect(rows, swap):
    if swap:
        rows = swap_quarters(rows)
    for mask in (2, 1) if swap else (1, 2):
        rows = halve(rows, mask)
    return rows


def block_of(extent, most):
    size = most
    while extent % size:
        size //= 2
    return size


def dot_f32(left, right, left_dim, right_dim):
    return lax.dot_general(
        left, right, (((left_dim,), (right_dim,)), ((), ())), preferred_element_type=jnp.float32
    )


def product_kernel(right_dim, left_ref, right_ref, out_ref):
    out_ref[...] = dot_f32(left_ref[...], right_ref[...], 1, right_dim).astype(out_ref.dtype)


def product(left, column_block, depth, right, transposed):
    height = left.shape[0]
    width = right.shape[0] if transposed else right.shape[1]
    step = block_of(width, 256)
    if transposed:
        right_spec = pl.BlockSpec((step, depth), lambda j: (j, 0))
    else:
        right_spec = pl.BlockSpec((depth, step), lambda j: (0, j))
    return pl.pallas_call(
        functools.partial(product_kernel, 1 if transposed else 0),
        grid=(width // step,),
        in_specs=[pl.BlockSpec((height, depth), lambda j: (0, column_block)), right_spec],
        out_specs=pl.BlockSpec((height, step), lambda j: (0, j)),
        out_shape=jax.ShapeDtypeStruct((height, width), jnp.bfloat16),
        compiler_params=pltpu.CompilerParams(vmem_limit_bytes=VMEM_BYTES),
        cost_estimate=pl.CostEstimate(
            flops=2 * height * depth * width,
            bytes_accessed=2 * (height * depth + depth * width + height * width),
            transcendentals=0,
        ),
    )(left, right)


def pair_over_grp(part):
    if lax.axis_size("grp") == 2:
        return part, lax.ppermute(part, "grp", [(0, 1), (1, 0)])
    return lax.psum(part, "grp"), jnp.zeros_like(part)


def finish_kernel(
    keep_ref, gate_a, gate_b, grad_a, grad_b, matrix_ref, out_ref, hidden_ref, branch_ref
):
    height, width = hidden_ref.shape

    @pl.when(pl.program_id(0) == 0)
    def _():
        keep = keep_ref[0] > 0
        step = block_of(height, 32)

        @pl.loop(0, height // step)
        def _(i):
            here = pl.ds(pl.multiple_of(i * step, step), step)

            def total(one, two, columns):
                return one[here, columns].astype(jnp.float32) + two[here, columns].astype(
                    jnp.float32
                )

            gate_value = total(gate_a, gate_b, pl.ds(0, width))
            upward = total(gate_a, gate_b, pl.ds(width, width))
            hidden_grads = total(grad_a, grad_b, pl.ds(0, width))
            sigmoid_value = jax.nn.sigmoid(gate_value)
            activated = gate_value * sigmoid_value
            gate_slope = sigmoid_value * (1.0 + gate_value * (1.0 - sigmoid_value))

            def put(ref, columns, value):
                ref[here, columns] = jnp.where(keep, value, 0.0).astype(ref.dtype)

            put(hidden_ref, pl.ds(0, width), activated * upward)
            put(branch_ref, pl.ds(0, width), hidden_grads * upward * gate_slope)
            put(branch_ref, pl.ds(width, width), hidden_grads * activated)

    out_ref[...] = dot_f32(branch_ref[...], matrix_ref[...], 1, 1).astype(out_ref.dtype)


def finish(keep, gate_pair, grad_pair, matrix):
    height, width = grad_pair[0].shape
    features = matrix.shape[0]
    step = block_of(features, 512)
    whole = lambda columns: pl.BlockSpec((height, columns), lambda j: (0, 0))
    shape = lambda columns: jax.ShapeDtypeStruct((height, columns), jnp.bfloat16)
    return pl.pallas_call(
        finish_kernel,
        grid=(features // step,),
        in_specs=[
            pl.BlockSpec(memory_space=pltpu.SMEM),
            whole(2 * width),
            whole(2 * width),
            whole(width),
            whole(width),
            pl.BlockSpec((step, 2 * width), lambda j: (j, 0)),
        ],
        out_specs=[
            pl.BlockSpec((height, step), lambda j: (0, j)),
            whole(width),
            whole(2 * width),
        ],
        out_shape=[shape(features), shape(width), shape(2 * width)],
        compiler_params=pltpu.CompilerParams(vmem_limit_bytes=VMEM_BYTES),
        cost_estimate=pl.CostEstimate(
            flops=4 * height * width * features,
            bytes_accessed=4 * width * features + 2 * height * (features + 9 * width),
            transcendentals=height * width,
        ),
    )(keep, *gate_pair, *grad_pair, matrix)


def outer(left, right):
    return lax.dot_general(
        left, right, (((0,), (0,)), ((), ())), preferred_element_type=jnp.float32
    ).astype(jnp.bfloat16)


def local(tokens, d_out, row_expert, w_gate_up, w_down):
    row_count, feature_share = tokens.shape
    hidden_width = w_down.shape[1]
    expert_count = lax.axis_size("exp")
    gate_up_matrix = w_gate_up.reshape(feature_share, 2 * hidden_width)
    down_matrix = w_down.reshape(hidden_width, feature_share)
    cap = 2 * row_count // expert_count
    half = cap // 2

    rank = rank_in_expert(row_expert)
    is_spill = rank >= cap
    busiest = jnp.max(jnp.where(is_spill, row_expert, -1))
    is_busiest = lax.axis_index("exp") == busiest
    spill_hot = one_hot(jnp.where(is_spill, rank - cap, -1), cap)
    chunk_hot = []
    for chunk in range(2):
        inside = (rank >= chunk * half) & (rank < (chunk + 1) * half)
        slot = row_expert * half + rank - chunk * half
        chunk_hot.append(one_hot(jnp.where(inside, slot, -1), expert_count * half))

    both = jnp.concatenate([tokens, d_out], axis=1)

    def split(both_in):
        return both_in[:, :feature_share], both_in[:, feature_share:]

    def step(keep, rows_in, rows_block, grads_in, grads_block):
        gate_pair = pair_over_grp(
            product(rows_in, rows_block, feature_share, gate_up_matrix, False)
        )
        grad_pair = pair_over_grp(
            product(grads_in, grads_block, feature_share, down_matrix, True)
        )
        return finish(keep, gate_pair, grad_pair, gate_up_matrix)

    always = jnp.ones((1,), jnp.int32)
    only_busiest = is_busiest.astype(jnp.int32).reshape(1)

    far = outer_masks()
    spill_both = place(spill_hot, both)
    for mask in far:
        spill_both = double(spill_both, mask)
    sent_0 = place(chunk_hot[0], both)
    spill_both, sent_0 = lax.optimization_barrier((spill_both, sent_0))

    arrived_0 = exchange(sent_0, expert_count)
    spill_rows, spill_grads = split(spill_both)
    spill_rows, spill_grads = spread(spill_rows, False), spread(spill_grads, True)
    sent_1 = place(chunk_hot[1], both)
    arrived_0, spill_rows, spill_grads, sent_1, gate_up_matrix = lax.optimization_barrier(
        (arrived_0, spill_rows, spill_grads, sent_1, gate_up_matrix)
    )

    arrived_1 = exchange(sent_1, expert_count)
    out_0, hidden_0, branch_0 = step(always, arrived_0, 0, arrived_0, 1)
    out_s, hidden_s, branch_s = step(only_busiest, spill_rows, 0, spill_grads, 0)
    rows_0, grads_0 = split(arrived_0)
    arrived_1, out_0, out_s = lax.optimization_barrier((arrived_1, out_0, out_s))

    back_0 = exchange(out_0, expert_count)
    middle = feature_share // 2
    back_s = jnp.concatenate(
        [collect(out_s[:, :middle], False), collect(out_s[:, middle:], True)], axis=1
    )
    out_1, hidden_1, branch_1 = step(always, arrived_1, 0, arrived_1, 1)
    rows_1, grads_1 = split(arrived_1)
    back_0, back_s, out_1 = lax.optimization_barrier((back_0, back_s, out_1))

    back_1 = exchange(out_1, expert_count)
    for mask in reversed(far):
        back_s = halve(back_s, mask)

    all_rows = jnp.concatenate([spill_rows, rows_0, rows_1], axis=0)
    all_grads = jnp.concatenate([spill_grads, grads_0, grads_1], axis=0)
    hidden = jnp.concatenate([hidden_s, hidden_0, hidden_1], axis=0)
    branch = jnp.concatenate([branch_s, branch_0, branch_1], axis=0)
    gate_up_grads = with_layout_constraint(outer(all_rows, branch), Layout((0, 1)))
    gate_up_grads = lax.optimization_barrier(
        gate_up_grads.reshape(feature_share // 8, 8, 2, hidden_width).transpose(0, 2, 1, 3)
    )
    gate_up_grads = gate_up_grads.transpose(0, 2, 1, 3).reshape(
        1, feature_share, 2, hidden_width
    )
    down_grads = outer(hidden, all_grads).reshape(1, hidden_width, feature_share)

    pick = jnp.concatenate([spill_hot] + chunk_hot, axis=0)
    returned = jnp.concatenate([back_s, back_0, back_1], axis=0)
    token_grads = lax.dot_general(
        pick, returned, (((0,), (0,)), ((), ())), preferred_element_type=jnp.float32
    ).astype(jnp.bfloat16)
    return (token_grads, gate_up_grads, down_grads)


def solution(mesh):
    return jax.shard_map(
        local,
        mesh=mesh,
        in_specs=(
            P("exp", "grp"),
            P("exp", "grp"),
            P("exp"),
            P("exp", "grp", None, None),
            P("exp", None, "grp"),
        ),
        out_specs=(P("exp", "grp"), P("exp", "grp", None, None), P("exp", None, "grp")),
        check_vma=False,
    )
```

```python
import functools

import jax
import jax.numpy as jnp
from jax import lax
from jax.experimental import pallas as pl
from jax.experimental.layout import Layout, with_layout_constraint
from jax.experimental.pallas import tpu as pltpu
from jax.sharding import PartitionSpec as P

VMEM_BYTES = 48 * 1024 * 1024


def rank_in_expert(row_expert):
    row_count = row_expert.shape[0]
    same = row_expert[:, None] == row_expert[None, :]
    earlier = jnp.arange(row_count)[None, :] < jnp.arange(row_count)[:, None]
    return jnp.sum((same & earlier).astype(jnp.int32), axis=1)


def one_hot(index, total):
    return (index[None, :] == jnp.arange(total, dtype=jnp.int32)[:, None]).astype(jnp.bfloat16)


def place(one_hot_rows, rows):
    return lax.dot_general(
        one_hot_rows, rows, (((1,), (0,)), ((), ())), preferred_element_type=jnp.float32
    ).astype(jnp.bfloat16)


def exchange(rows, expert_count):
    slots, width = rows.shape
    return lax.all_to_all(
        rows.reshape(expert_count, slots // expert_count, width),
        "exp",
        split_axis=0,
        concat_axis=0,
        tiled=True,
    ).reshape(slots, width)


def swap_with(rows, mask):
    total = lax.axis_size("exp")
    return lax.ppermute(rows, "exp", [(i, i ^ mask) for i in range(total)])


def double(rows, mask):
    return jnp.concatenate([rows, swap_with(rows, mask)], axis=0)


def halves(rows):
    half = rows.shape[0] // 2
    return rows[:half], rows[half:]


def halve(rows, mask):
    kept, sent = halves(rows)
    return kept + swap_with(sent, mask)


def outer_masks():
    masks = []
    bit = lax.axis_size("exp") // 2
    while bit > 2:
        masks.append(bit)
        bit //= 2
    return masks


def swap_quarters(rows):
    quarter = rows.shape[0] // 4
    parts = [rows[i * quarter : (i + 1) * quarter] for i in (0, 2, 1, 3)]
    return jnp.concatenate(parts, axis=0)


def block_of(extent, most):
    size = most
    while extent % size:
        size //= 2
    return size


def dot_f32(left, right, left_dim, right_dim):
    return lax.dot_general(
        left, right, (((left_dim,), (right_dim,)), ((), ())), preferred_element_type=jnp.float32
    )


def product_kernel(right_dim, left_ref, right_ref, out_ref):
    out_ref[...] = dot_f32(left_ref[...], right_ref[...], 1, right_dim).astype(out_ref.dtype)


def product(left, column_block, depth, right, transposed):
    height = left.shape[0]
    width = right.shape[0] if transposed else right.shape[1]
    step = block_of(width, 256)
    if transposed:
        right_spec = pl.BlockSpec((step, depth), lambda j: (j, 0))
    else:
        right_spec = pl.BlockSpec((depth, step), lambda j: (0, j))
    return pl.pallas_call(
        functools.partial(product_kernel, 1 if transposed else 0),
        grid=(width // step,),
        in_specs=[pl.BlockSpec((height, depth), lambda j: (0, column_block)), right_spec],
        out_specs=pl.BlockSpec((height, step), lambda j: (0, j)),
        out_shape=jax.ShapeDtypeStruct((height, width), jnp.bfloat16),
        compiler_params=pltpu.CompilerParams(vmem_limit_bytes=VMEM_BYTES),
        cost_estimate=pl.CostEstimate(
            flops=2 * height * depth * width,
            bytes_accessed=2 * (height * depth + depth * width + height * width),
            transcendentals=0,
        ),
    )(left, right)


def pair_over_grp(part):
    if lax.axis_size("grp") == 2:
        return part, lax.ppermute(part, "grp", [(0, 1), (1, 0)])
    return lax.psum(part, "grp"), jnp.zeros_like(part)


def finish_kernel(
    keep_ref, gate_a, gate_b, grad_a, grad_b, matrix_ref, out_ref, hidden_ref, branch_ref
):
    height, width = hidden_ref.shape

    @pl.when(pl.program_id(0) == 0)
    def _():
        keep = keep_ref[0] > 0
        step = block_of(height, 32)

        @pl.loop(0, height // step)
        def _(i):
            here = pl.ds(pl.multiple_of(i * step, step), step)

            def total(one, two, columns):
                return one[here, columns].astype(jnp.float32) + two[here, columns].astype(
                    jnp.float32
                )

            gate_value = total(gate_a, gate_b, pl.ds(0, width))
            upward = total(gate_a, gate_b, pl.ds(width, width))
            hidden_grads = total(grad_a, grad_b, pl.ds(0, width))
            sigmoid_value = jax.nn.sigmoid(gate_value)
            activated = gate_value * sigmoid_value
            gate_slope = sigmoid_value * (1.0 + gate_value * (1.0 - sigmoid_value))

            def put(ref, columns, value):
                ref[here, columns] = jnp.where(keep, value, 0.0).astype(ref.dtype)

            put(hidden_ref, pl.ds(0, width), activated * upward)
            put(branch_ref, pl.ds(0, width), hidden_grads * upward * gate_slope)
            put(branch_ref, pl.ds(width, width), hidden_grads * activated)

    out_ref[...] = dot_f32(branch_ref[...], matrix_ref[...], 1, 1).astype(out_ref.dtype)


def finish(keep, gate_pair, grad_pair, matrix):
    height, width = grad_pair[0].shape
    features = matrix.shape[0]
    step = block_of(features, 512)
    whole = lambda columns: pl.BlockSpec((height, columns), lambda j: (0, 0))
    shape = lambda columns: jax.ShapeDtypeStruct((height, columns), jnp.bfloat16)
    return pl.pallas_call(
        finish_kernel,
        grid=(features // step,),
        in_specs=[
            pl.BlockSpec(memory_space=pltpu.SMEM),
            whole(2 * width),
            whole(2 * width),
            whole(width),
            whole(width),
            pl.BlockSpec((step, 2 * width), lambda j: (j, 0)),
        ],
        out_specs=[
            pl.BlockSpec((height, step), lambda j: (0, j)),
            whole(width),
            whole(2 * width),
        ],
        out_shape=[shape(features), shape(width), shape(2 * width)],
        compiler_params=pltpu.CompilerParams(vmem_limit_bytes=VMEM_BYTES),
        cost_estimate=pl.CostEstimate(
            flops=4 * height * width * features,
            bytes_accessed=4 * width * features + 2 * height * (features + 9 * width),
            transcendentals=height * width,
        ),
    )(keep, *gate_pair, *grad_pair, matrix)


def outer(left, right):
    return lax.dot_general(
        left, right, (((0,), (0,)), ((), ())), preferred_element_type=jnp.float32
    ).astype(jnp.bfloat16)


def local(tokens, d_out, row_expert, w_gate_up, w_down):
    row_count, feature_share = tokens.shape
    hidden_width = w_down.shape[1]
    expert_count = lax.axis_size("exp")
    gate_up_matrix = w_gate_up.reshape(feature_share, 2 * hidden_width)
    down_matrix = w_down.reshape(hidden_width, feature_share)
    cap = 2 * row_count // expert_count
    half = cap // 2

    rank = rank_in_expert(row_expert)
    is_spill = rank >= cap
    busiest = jnp.max(jnp.where(is_spill, row_expert, -1))
    is_busiest = lax.axis_index("exp") == busiest
    spill_hot = one_hot(jnp.where(is_spill, rank - cap, -1), cap)
    chunk_hot = []
    for chunk in range(2):
        inside = (rank >= chunk * half) & (rank < (chunk + 1) * half)
        slot = row_expert * half + rank - chunk * half
        chunk_hot.append(one_hot(jnp.where(inside, slot, -1), expert_count * half))

    both = jnp.concatenate([tokens, d_out], axis=1)

    def split(both_in):
        return both_in[:, :feature_share], both_in[:, feature_share:]

    def step(keep, rows_in, rows_block, grads_in, grads_block):
        gate_pair = pair_over_grp(
            product(rows_in, rows_block, feature_share, gate_up_matrix, False)
        )
        grad_pair = pair_over_grp(
            product(grads_in, grads_block, feature_share, down_matrix, True)
        )
        return finish(keep, gate_pair, grad_pair, gate_up_matrix)

    always = jnp.ones((1,), jnp.int32)
    only_busiest = is_busiest.astype(jnp.int32).reshape(1)

    far = outer_masks()
    spill_both = double(place(spill_hot, both), far[0])
    spill_both, hot_0 = lax.optimization_barrier((spill_both, chunk_hot[0]))

    arrived_0 = exchange(place(hot_0, both), expert_count)
    for mask in far[1:]:
        spill_both = double(spill_both, mask)
    spill_rows, spill_grads = split(spill_both)
    spill_rows, spill_grads = double(spill_rows, 2), double(spill_grads, 1)
    arrived_0, spill_rows, spill_grads, hot_1, gate_up_matrix = lax.optimization_barrier(
        (arrived_0, spill_rows, spill_grads, chunk_hot[1], gate_up_matrix)
    )

    arrived_1 = exchange(place(hot_1, both), expert_count)
    spill_rows, spill_grads = double(spill_rows, 1), swap_quarters(double(spill_grads, 2))
    out_0, hidden_0, branch_0 = step(always, arrived_0, 0, arrived_0, 1)
    out_s, hidden_s, branch_s = step(only_busiest, spill_rows, 0, spill_grads, 0)
    rows_0, grads_0 = split(arrived_0)
    middle = feature_share // 2
    kept_a, sent_a = halves(out_s[:, :middle])
    kept_b, sent_b = halves(swap_quarters(out_s[:, middle:]))
    arrived_1, out_0, kept_a, sent_a, kept_b, sent_b = lax.optimization_barrier(
        (arrived_1, out_0, kept_a, sent_a, kept_b, sent_b)
    )

    back_0 = exchange(out_0, expert_count)
    back_a = kept_a + swap_with(sent_a, 1)
    back_b = kept_b + swap_with(sent_b, 2)
    out_1, hidden_1, branch_1 = step(always, arrived_1, 0, arrived_1, 1)
    back_0, back_a, back_b, out_1, arrived_1 = lax.optimization_barrier(
        (back_0, back_a, back_b, out_1, arrived_1)
    )

    back_1 = exchange(out_1, expert_count)
    back_s = jnp.concatenate([halve(back_a, 2), halve(back_b, 1)], axis=1)
    for mask in reversed(far[1:]):
        back_s = halve(back_s, mask)
    rows_1, grads_1 = split(arrived_1)

    all_rows = jnp.concatenate([spill_rows, rows_0, rows_1], axis=0)
    all_grads = jnp.concatenate([spill_grads, grads_0, grads_1], axis=0)
    hidden = jnp.concatenate([hidden_s, hidden_0, hidden_1], axis=0)
    branch = jnp.concatenate([branch_s, branch_0, branch_1], axis=0)
    gate_up_grads = with_layout_constraint(outer(all_rows, branch), Layout((0, 1)))
    gate_up_grads = lax.optimization_barrier(
        gate_up_grads.reshape(feature_share // 8, 8, 2, hidden_width).transpose(0, 2, 1, 3)
    )
    gate_up_grads = gate_up_grads.transpose(0, 2, 1, 3).reshape(
        1, feature_share, 2, hidden_width
    )
    down_grads = outer(hidden, all_grads).reshape(1, hidden_width, feature_share)

    back_s, gate_up_grads, down_grads = lax.optimization_barrier(
        (back_s, gate_up_grads, down_grads)
    )
    back_s = halve(back_s, far[0])

    pick = jnp.concatenate([spill_hot] + chunk_hot, axis=0)
    returned = jnp.concatenate([back_s, back_0, back_1], axis=0)
    token_grads = lax.dot_general(
        pick, returned, (((0,), (0,)), ((), ())), preferred_element_type=jnp.float32
    ).astype(jnp.bfloat16)
    return (token_grads, gate_up_grads, down_grads)


def solution(mesh):
    return jax.shard_map(
        local,
        mesh=mesh,
        in_specs=(
            P("exp", "grp"),
            P("exp", "grp"),
            P("exp"),
            P("exp", "grp", None, None),
            P("exp", None, "grp"),
        ),
        out_specs=(P("exp", "grp"), P("exp", "grp", None, None), P("exp", None, "grp")),
        check_vma=False,
    )
```

```python
import functools

import jax
import jax.numpy as jnp
from jax import lax
from jax.experimental import pallas as pl
from jax.experimental.layout import Layout, with_layout_constraint
from jax.experimental.pallas import tpu as pltpu
from jax.sharding import PartitionSpec as P

VMEM_BYTES = 48 * 1024 * 1024
SMALL_COST = pl.CostEstimate(flops=1, bytes_accessed=1, transcendentals=0)


def rank_in_expert(row_expert):
    row_count = row_expert.shape[0]
    same = row_expert[:, None] == row_expert[None, :]
    earlier = jnp.arange(row_count)[None, :] < jnp.arange(row_count)[:, None]
    return jnp.sum((same & earlier).astype(jnp.int32), axis=1)


def one_hot(index, total):
    return (index[None, :] == jnp.arange(total, dtype=jnp.int32)[:, None]).astype(jnp.bfloat16)


def place(one_hot_rows, rows):
    return lax.dot_general(
        one_hot_rows, rows, (((1,), (0,)), ((), ())), preferred_element_type=jnp.float32
    ).astype(jnp.bfloat16)


def exchange(rows, expert_count):
    slots, width = rows.shape
    return lax.all_to_all(
        rows.reshape(expert_count, slots // expert_count, width),
        "exp",
        split_axis=0,
        concat_axis=0,
        tiled=True,
    ).reshape(slots, width)


def swap_with(rows, mask):
    total = lax.axis_size("exp")
    return lax.ppermute(rows, "exp", [(i, i ^ mask) for i in range(total)])


def double(rows, mask):
    return jnp.concatenate([rows, swap_with(rows, mask)], axis=0)


def halves(rows):
    half = rows.shape[0] // 2
    return rows[:half], rows[half:]


def halve(rows, mask):
    kept, sent = halves(rows)
    return kept + swap_with(sent, mask)


def outer_masks():
    masks = []
    bit = lax.axis_size("exp") // 2
    while bit > 2:
        masks.append(bit)
        bit //= 2
    return masks


def swap_quarters(rows):
    quarter = rows.shape[0] // 4
    parts = [rows[i * quarter : (i + 1) * quarter] for i in (0, 2, 1, 3)]
    return jnp.concatenate(parts, axis=0)


def block_of(extent, most):
    size = most
    while extent % size:
        size //= 2
    return size


def dot_f32(left, right, left_dim, right_dim):
    return lax.dot_general(
        left, right, (((left_dim,), (right_dim,)), ((), ())), preferred_element_type=jnp.float32
    )


def product_kernel(right_dim, left_ref, right_ref, out_ref):
    out_ref[...] = dot_f32(left_ref[...], right_ref[...], 1, right_dim).astype(out_ref.dtype)


def product(left, column_block, depth, right, transposed):
    height = left.shape[0]
    width = right.shape[0] if transposed else right.shape[1]
    step = block_of(width, 256)
    if transposed:
        right_spec = pl.BlockSpec((step, depth), lambda j: (j, 0))
    else:
        right_spec = pl.BlockSpec((depth, step), lambda j: (0, j))
    return pl.pallas_call(
        functools.partial(product_kernel, 1 if transposed else 0),
        grid=(width // step,),
        in_specs=[pl.BlockSpec((height, depth), lambda j: (0, column_block)), right_spec],
        out_specs=pl.BlockSpec((height, step), lambda j: (0, j)),
        out_shape=jax.ShapeDtypeStruct((height, width), jnp.bfloat16),
        compiler_params=pltpu.CompilerParams(vmem_limit_bytes=VMEM_BYTES),
        cost_estimate=SMALL_COST,
    )(left, right)


def pair_over_grp(part):
    if lax.axis_size("grp") == 2:
        return part, lax.ppermute(part, "grp", [(0, 1), (1, 0)])
    return lax.psum(part, "grp"), jnp.zeros_like(part)


def finish_kernel(
    keep_ref, gate_a, gate_b, grad_a, grad_b, matrix_ref, out_ref, hidden_ref, branch_ref
):
    height, width = hidden_ref.shape

    @pl.when(pl.program_id(0) == 0)
    def _():
        keep = keep_ref[0] > 0
        step = block_of(height, 32)

        @pl.loop(0, height // step)
        def _(i):
            here = pl.ds(pl.multiple_of(i * step, step), step)

            def total(one, two, columns):
                return one[here, columns].astype(jnp.float32) + two[here, columns].astype(
                    jnp.float32
                )

            gate_value = total(gate_a, gate_b, pl.ds(0, width))
            upward = total(gate_a, gate_b, pl.ds(width, width))
            hidden_grads = total(grad_a, grad_b, pl.ds(0, width))
            sigmoid_value = jax.nn.sigmoid(gate_value)
            activated = gate_value * sigmoid_value
            gate_slope = sigmoid_value * (1.0 + gate_value * (1.0 - sigmoid_value))

            def put(ref, columns, value):
                ref[here, columns] = jnp.where(keep, value, 0.0).astype(ref.dtype)

            put(hidden_ref, pl.ds(0, width), activated * upward)
            put(branch_ref, pl.ds(0, width), hidden_grads * upward * gate_slope)
            put(branch_ref, pl.ds(width, width), hidden_grads * activated)

    out_ref[...] = dot_f32(branch_ref[...], matrix_ref[...], 1, 1).astype(out_ref.dtype)


def finish(keep, gate_pair, grad_pair, matrix):
    height, width = grad_pair[0].shape
    features = matrix.shape[0]
    step = block_of(features, 512)
    whole = lambda columns: pl.BlockSpec((height, columns), lambda j: (0, 0))
    shape = lambda columns: jax.ShapeDtypeStruct((height, columns), jnp.bfloat16)
    return pl.pallas_call(
        finish_kernel,
        grid=(features // step,),
        in_specs=[
            pl.BlockSpec(memory_space=pltpu.SMEM),
            whole(2 * width),
            whole(2 * width),
            whole(width),
            whole(width),
            pl.BlockSpec((step, 2 * width), lambda j: (j, 0)),
        ],
        out_specs=[
            pl.BlockSpec((height, step), lambda j: (0, j)),
            whole(width),
            whole(2 * width),
        ],
        out_shape=[shape(features), shape(width), shape(2 * width)],
        compiler_params=pltpu.CompilerParams(vmem_limit_bytes=VMEM_BYTES),
        cost_estimate=SMALL_COST,
    )(keep, *gate_pair, *grad_pair, matrix)


def outer(left, right):
    return lax.dot_general(
        left, right, (((0,), (0,)), ((), ())), preferred_element_type=jnp.float32
    ).astype(jnp.bfloat16)


def local(tokens, d_out, row_expert, w_gate_up, w_down):
    row_count, feature_share = tokens.shape
    hidden_width = w_down.shape[1]
    expert_count = lax.axis_size("exp")
    gate_up_matrix = w_gate_up.reshape(feature_share, 2 * hidden_width)
    down_matrix = w_down.reshape(hidden_width, feature_share)
    cap = 2 * row_count // expert_count
    bounds = (0, cap // 4, cap)

    rank = rank_in_expert(row_expert)
    is_spill = rank >= cap
    busiest = jnp.max(jnp.where(is_spill, row_expert, -1))
    is_busiest = lax.axis_index("exp") == busiest
    spill_hot = one_hot(jnp.where(is_spill, rank - cap, -1), cap)
    chunk_hot = []
    for low, high in zip(bounds, bounds[1:]):
        inside = (rank >= low) & (rank < high)
        slot = row_expert * (high - low) + rank - low
        chunk_hot.append(one_hot(jnp.where(inside, slot, -1), expert_count * (high - low)))

    both = jnp.concatenate([tokens, d_out], axis=1)

    def split(both_in):
        return both_in[:, :feature_share], both_in[:, feature_share:]

    def step(keep, rows_in, rows_block, grads_in, grads_block):
        gate_pair = pair_over_grp(
            product(rows_in, rows_block, feature_share, gate_up_matrix, False)
        )
        grad_pair = pair_over_grp(
            product(grads_in, grads_block, feature_share, down_matrix, True)
        )
        return finish(keep, gate_pair, grad_pair, gate_up_matrix)

    always = jnp.ones((1,), jnp.int32)
    only_busiest = is_busiest.astype(jnp.int32).reshape(1)

    far = outer_masks()
    spill_both = place(spill_hot, both)
    for mask in far:
        spill_both = double(spill_both, mask)
    spill_rows, spill_grads = split(spill_both)
    sent_0 = place(chunk_hot[0], both)
    spill_rows, spill_grads, sent_0 = lax.optimization_barrier((spill_rows, spill_grads, sent_0))

    arrived_0 = exchange(sent_0, expert_count)
    spill_rows, spill_grads = double(spill_rows, 2), double(spill_grads, 1)
    sent_1 = place(chunk_hot[1], both)
    arrived_0, spill_rows, spill_grads, sent_1, gate_up_matrix = lax.optimization_barrier(
        (arrived_0, spill_rows, spill_grads, sent_1, gate_up_matrix)
    )

    arrived_1 = exchange(sent_1, expert_count)
    spill_rows, spill_grads = double(spill_rows, 1), swap_quarters(double(spill_grads, 2))
    out_0, hidden_0, branch_0 = step(always, arrived_0, 0, arrived_0, 1)
    out_s, hidden_s, branch_s = step(only_busiest, spill_rows, 0, spill_grads, 0)
    rows_0, grads_0 = split(arrived_0)
    middle = feature_share // 2
    kept_a, sent_a = halves(out_s[:, :middle])
    kept_b, sent_b = halves(swap_quarters(out_s[:, middle:]))
    arrived_1, out_0, kept_a, sent_a, kept_b, sent_b = lax.optimization_barrier(
        (arrived_1, out_0, kept_a, sent_a, kept_b, sent_b)
    )

    back_0 = exchange(out_0, expert_count)
    come_a = swap_with(sent_a, 1)
    come_b = swap_with(sent_b, 2)
    out_1, hidden_1, branch_1 = step(always, arrived_1, 0, arrived_1, 1)
    back_0, come_a, come_b, out_1, arrived_1 = lax.optimization_barrier(
        (back_0, come_a, come_b, out_1, arrived_1)
    )

    back_1 = exchange(out_1, expert_count)
    back_s = jnp.concatenate([halve(kept_a + come_a, 2), halve(kept_b + come_b, 1)], axis=1)
    for mask in reversed(far[1:]):
        back_s = halve(back_s, mask)
    rows_1, grads_1 = split(arrived_1)

    all_rows = jnp.concatenate([spill_rows, rows_0, rows_1], axis=0)
    all_grads = jnp.concatenate([spill_grads, grads_0, grads_1], axis=0)
    hidden = jnp.concatenate([hidden_s, hidden_0, hidden_1], axis=0)
    branch = jnp.concatenate([branch_s, branch_0, branch_1], axis=0)
    gate_up_grads = with_layout_constraint(outer(all_rows, branch), Layout((0, 1)))
    down_grads = outer(hidden, all_grads).reshape(1, hidden_width, feature_share)
    gate_up_grads = gate_up_grads.reshape(feature_share // 8, 8, 2, hidden_width)
    back_s, gate_up_grads, down_grads = lax.optimization_barrier(
        (back_s, gate_up_grads.transpose(0, 2, 1, 3), down_grads)
    )

    back_s = halve(back_s, far[0])
    gate_up_grads = gate_up_grads.transpose(0, 2, 1, 3).reshape(
        1, feature_share, 2, hidden_width
    )

    pick = jnp.concatenate([spill_hot] + chunk_hot, axis=0)
    returned = jnp.concatenate([back_s, back_0, back_1], axis=0)
    token_grads = lax.dot_general(
        pick, returned, (((0,), (0,)), ((), ())), preferred_element_type=jnp.float32
    ).astype(jnp.bfloat16)
    return (token_grads, gate_up_grads, down_grads)


def solution(mesh):
    return jax.shard_map(
        local,
        mesh=mesh,
        in_specs=(
            P("exp", "grp"),
            P("exp", "grp"),
            P("exp"),
            P("exp", "grp", None, None),
            P("exp", None, "grp"),
        ),
        out_specs=(P("exp", "grp"), P("exp", "grp", None, None), P("exp", None, "grp")),
        check_vma=False,
    )
```

```python
import functools

import jax
import jax.numpy as jnp
from jax import lax
from jax.experimental import pallas as pl
from jax.experimental.layout import Layout, with_layout_constraint
from jax.experimental.pallas import tpu as pltpu
from jax.sharding import PartitionSpec as P

VMEM_BYTES = 48 * 1024 * 1024
SMALL_COST = pl.CostEstimate(flops=1, bytes_accessed=1, transcendentals=0)


def rank_in_expert(row_expert):
    row_count = row_expert.shape[0]
    same = row_expert[:, None] == row_expert[None, :]
    earlier = jnp.arange(row_count)[None, :] < jnp.arange(row_count)[:, None]
    return jnp.sum((same & earlier).astype(jnp.int32), axis=1)


def one_hot(index, total):
    return (index[None, :] == jnp.arange(total, dtype=jnp.int32)[:, None]).astype(jnp.bfloat16)


def place(one_hot_rows, rows):
    return lax.dot_general(
        one_hot_rows, rows, (((1,), (0,)), ((), ())), preferred_element_type=jnp.float32
    ).astype(jnp.bfloat16)


def exchange(rows, expert_count):
    slots, width = rows.shape
    return lax.all_to_all(
        rows.reshape(expert_count, slots // expert_count, width),
        "exp",
        split_axis=0,
        concat_axis=0,
        tiled=True,
    ).reshape(slots, width)


def swap_with(rows, mask):
    total = lax.axis_size("exp")
    return lax.ppermute(rows, "exp", [(i, i ^ mask) for i in range(total)])


def double(rows, mask):
    return jnp.concatenate([rows, swap_with(rows, mask)], axis=0)


def halves(rows):
    half = rows.shape[0] // 2
    return rows[:half], rows[half:]


def halve(rows, mask):
    kept, sent = halves(rows)
    return kept + swap_with(sent, mask)


def outer_masks():
    masks = []
    bit = lax.axis_size("exp") // 2
    while bit > 2:
        masks.append(bit)
        bit //= 2
    return masks


def swap_quarters(rows):
    quarter = rows.shape[0] // 4
    parts = [rows[i * quarter : (i + 1) * quarter] for i in (0, 2, 1, 3)]
    return jnp.concatenate(parts, axis=0)


def block_of(extent, most):
    size = most
    while extent % size:
        size //= 2
    return size


def dot_f32(left, right, left_dim, right_dim):
    return lax.dot_general(
        left, right, (((left_dim,), (right_dim,)), ((), ())), preferred_element_type=jnp.float32
    )


def product_kernel(right_dim, left_ref, right_ref, out_ref):
    out_ref[...] = dot_f32(left_ref[...], right_ref[...], 1, right_dim).astype(out_ref.dtype)


def product(left, column_block, depth, right, transposed):
    height = left.shape[0]
    width = right.shape[0] if transposed else right.shape[1]
    step = block_of(width, 256)
    if transposed:
        right_spec = pl.BlockSpec((step, depth), lambda j: (j, 0))
    else:
        right_spec = pl.BlockSpec((depth, step), lambda j: (0, j))
    return pl.pallas_call(
        functools.partial(product_kernel, 1 if transposed else 0),
        grid=(width // step,),
        in_specs=[pl.BlockSpec((height, depth), lambda j: (0, column_block)), right_spec],
        out_specs=pl.BlockSpec((height, step), lambda j: (0, j)),
        out_shape=jax.ShapeDtypeStruct((height, width), jnp.bfloat16),
        compiler_params=pltpu.CompilerParams(vmem_limit_bytes=VMEM_BYTES),
        cost_estimate=SMALL_COST,
    )(left, right)


def pair_over_grp(part):
    if lax.axis_size("grp") == 2:
        return part, lax.ppermute(part, "grp", [(0, 1), (1, 0)])
    return lax.psum(part, "grp"), jnp.zeros_like(part)


def finish_kernel(
    keep_ref, gate_a, gate_b, grad_a, grad_b, matrix_ref, out_ref, hidden_ref, branch_ref
):
    height, width = hidden_ref.shape

    @pl.when(pl.program_id(0) == 0)
    def _():
        keep = keep_ref[0] > 0
        step = block_of(height, 32)

        @pl.loop(0, height // step)
        def _(i):
            here = pl.ds(pl.multiple_of(i * step, step), step)

            def total(one, two, columns):
                return one[here, columns].astype(jnp.float32) + two[here, columns].astype(
                    jnp.float32
                )

            gate_value = total(gate_a, gate_b, pl.ds(0, width))
            upward = total(gate_a, gate_b, pl.ds(width, width))
            hidden_grads = total(grad_a, grad_b, pl.ds(0, width))
            sigmoid_value = jax.nn.sigmoid(gate_value)
            activated = gate_value * sigmoid_value
            gate_slope = sigmoid_value * (1.0 + gate_value * (1.0 - sigmoid_value))

            def put(ref, columns, value):
                ref[here, columns] = jnp.where(keep, value, 0.0).astype(ref.dtype)

            put(hidden_ref, pl.ds(0, width), activated * upward)
            put(branch_ref, pl.ds(0, width), hidden_grads * upward * gate_slope)
            put(branch_ref, pl.ds(width, width), hidden_grads * activated)

    out_ref[...] = dot_f32(branch_ref[...], matrix_ref[...], 1, 1).astype(out_ref.dtype)


def finish(keep, gate_pair, grad_pair, matrix):
    height, width = grad_pair[0].shape
    features = matrix.shape[0]
    step = block_of(features, 512)
    whole = lambda columns: pl.BlockSpec((height, columns), lambda j: (0, 0))
    shape = lambda columns: jax.ShapeDtypeStruct((height, columns), jnp.bfloat16)
    return pl.pallas_call(
        finish_kernel,
        grid=(features // step,),
        in_specs=[
            pl.BlockSpec(memory_space=pltpu.SMEM),
            whole(2 * width),
            whole(2 * width),
            whole(width),
            whole(width),
            pl.BlockSpec((step, 2 * width), lambda j: (j, 0)),
        ],
        out_specs=[
            pl.BlockSpec((height, step), lambda j: (0, j)),
            whole(width),
            whole(2 * width),
        ],
        out_shape=[shape(features), shape(width), shape(2 * width)],
        compiler_params=pltpu.CompilerParams(vmem_limit_bytes=VMEM_BYTES),
        cost_estimate=SMALL_COST,
    )(keep, *gate_pair, *grad_pair, matrix)


def outer(left, right):
    return lax.dot_general(
        left, right, (((0,), (0,)), ((), ())), preferred_element_type=jnp.float32
    ).astype(jnp.bfloat16)


def local(tokens, d_out, row_expert, w_gate_up, w_down):
    row_count, feature_share = tokens.shape
    hidden_width = w_down.shape[1]
    expert_count = lax.axis_size("exp")
    gate_up_matrix = w_gate_up.reshape(feature_share, 2 * hidden_width)
    down_matrix = w_down.reshape(hidden_width, feature_share)
    cap = 2 * row_count // expert_count
    bounds = (0, cap // 4, cap)

    rank = rank_in_expert(row_expert)
    is_spill = rank >= cap
    busiest = jnp.max(jnp.where(is_spill, row_expert, -1))
    is_busiest = lax.axis_index("exp") == busiest
    spill_hot = one_hot(jnp.where(is_spill, rank - cap, -1), cap)
    chunk_hot = []
    for low, high in zip(bounds, bounds[1:]):
        inside = (rank >= low) & (rank < high)
        slot = row_expert * (high - low) + rank - low
        chunk_hot.append(one_hot(jnp.where(inside, slot, -1), expert_count * (high - low)))

    both = jnp.concatenate([tokens, d_out], axis=1)

    def split(both_in):
        return both_in[:, :feature_share], both_in[:, feature_share:]

    def products(rows_in, rows_block, grads_in, grads_block):
        gate_part = product(rows_in, rows_block, feature_share, gate_up_matrix, False)
        grad_part = product(grads_in, grads_block, feature_share, down_matrix, True)
        return pair_over_grp(gate_part), pair_over_grp(grad_part)

    always = jnp.ones((1,), jnp.int32)
    only_busiest = is_busiest.astype(jnp.int32).reshape(1)

    far = outer_masks()
    spill_both = place(spill_hot, both)
    for mask in far:
        spill_both = double(spill_both, mask)
    spill_rows, spill_grads = split(spill_both)
    sent_0 = place(chunk_hot[0], both)
    spill_rows, spill_grads, sent_0 = lax.optimization_barrier((spill_rows, spill_grads, sent_0))

    arrived_0 = exchange(sent_0, expert_count)
    spill_rows, spill_grads = double(spill_rows, 2), double(spill_grads, 1)
    arrived_0, spill_rows, spill_grads, hot_1, gate_up_matrix = lax.optimization_barrier(
        (arrived_0, spill_rows, spill_grads, chunk_hot[1], gate_up_matrix)
    )

    come_rows, come_grads = swap_with(spill_rows, 1), swap_with(spill_grads, 2)
    arrived_0, sent_1 = lax.optimization_barrier((arrived_0, place(hot_1, both)))
    arrived_1 = exchange(sent_1, expert_count)
    out_0, hidden_0, branch_0 = finish(
        always, *products(arrived_0, 0, arrived_0, 1), gate_up_matrix
    )
    rows_0, grads_0 = split(arrived_0)
    come_rows, come_grads, out_0, rows_0, grads_0 = lax.optimization_barrier(
        (come_rows, come_grads, out_0, rows_0, grads_0)
    )
    spill_rows = jnp.concatenate([spill_rows, come_rows], axis=0)
    spill_grads = swap_quarters(jnp.concatenate([spill_grads, come_grads], axis=0))
    out_s, hidden_s, branch_s = finish(
        only_busiest, *products(spill_rows, 0, spill_grads, 0), gate_up_matrix
    )
    middle = feature_share // 2
    kept_a, sent_a = halves(out_s[:, :middle])
    kept_b, sent_b = halves(swap_quarters(out_s[:, middle:]))
    arrived_1, out_0, kept_a, sent_a, kept_b, sent_b = lax.optimization_barrier(
        (arrived_1, out_0, kept_a, sent_a, kept_b, sent_b)
    )

    back_0 = exchange(out_0, expert_count)
    come_a, come_b = swap_with(sent_a, 1), swap_with(sent_b, 2)
    come_a, come_b, gate_pair, grad_pair = lax.optimization_barrier(
        (come_a, come_b, *products(arrived_1, 0, arrived_1, 1))
    )
    kept_a, sent_a = halves(kept_a + come_a)
    kept_b, sent_b = halves(kept_b + come_b)
    come_a, come_b = swap_with(sent_a, 2), swap_with(sent_b, 1)
    out_1, hidden_1, branch_1 = finish(always, gate_pair, grad_pair, gate_up_matrix)
    come_a, come_b, out_1 = lax.optimization_barrier((come_a, come_b, out_1))
    back_s = jnp.concatenate([kept_a + come_a, kept_b + come_b], axis=1)
    back_0, back_s, out_1, arrived_1 = lax.optimization_barrier(
        (back_0, back_s, out_1, arrived_1)
    )

    for mask in reversed(far[1:]):
        back_s = halve(back_s, mask)
    rows_1, grads_1 = split(arrived_1)
    out_1, rows_1 = lax.optimization_barrier((out_1, rows_1))
    back_1 = exchange(out_1, expert_count)

    all_rows = jnp.concatenate([spill_rows, rows_0, rows_1], axis=0)
    all_grads = jnp.concatenate([spill_grads, grads_0, grads_1], axis=0)
    hidden = jnp.concatenate([hidden_s, hidden_0, hidden_1], axis=0)
    branch = jnp.concatenate([branch_s, branch_0, branch_1], axis=0)
    gate_up_grads = with_layout_constraint(outer(all_rows, branch), Layout((0, 1)))
    down_grads = outer(hidden, all_grads).reshape(1, hidden_width, feature_share)
    gate_up_grads = gate_up_grads.reshape(feature_share // 8, 8, 2, hidden_width)
    back_s, gate_up_grads, down_grads = lax.optimization_barrier(
        (back_s, gate_up_grads.transpose(0, 2, 1, 3), down_grads)
    )

    back_s = halve(back_s, far[0])
    gate_up_grads = gate_up_grads.transpose(0, 2, 1, 3).reshape(
        1, feature_share, 2, hidden_width
    )

    pick = jnp.concatenate([spill_hot] + chunk_hot, axis=0)
    returned = jnp.concatenate([back_s, back_0, back_1], axis=0)
    token_grads = lax.dot_general(
        pick, returned, (((0,), (0,)), ((), ())), preferred_element_type=jnp.float32
    ).astype(jnp.bfloat16)
    return (token_grads, gate_up_grads, down_grads)


def solution(mesh):
    return jax.shard_map(
        local,
        mesh=mesh,
        in_specs=(
            P("exp", "grp"),
            P("exp", "grp"),
            P("exp"),
            P("exp", "grp", None, None),
            P("exp", None, "grp"),
        ),
        out_specs=(P("exp", "grp"), P("exp", "grp", None, None), P("exp", None, "grp")),
        check_vma=False,
    )
```

```python
import functools

import jax
import jax.numpy as jnp
from jax import lax
from jax.experimental import pallas as pl
from jax.experimental.layout import Layout, with_layout_constraint
from jax.experimental.pallas import tpu as pltpu
from jax.sharding import PartitionSpec as P

VMEM_BYTES = 48 * 1024 * 1024
SMALL_COST = pl.CostEstimate(flops=1, bytes_accessed=1, transcendentals=0)


def rank_in_expert(row_expert):
    row_count = row_expert.shape[0]
    same = row_expert[:, None] == row_expert[None, :]
    earlier = jnp.arange(row_count)[None, :] < jnp.arange(row_count)[:, None]
    return jnp.sum((same & earlier).astype(jnp.int32), axis=1)


def one_hot(index, total):
    return (index[None, :] == jnp.arange(total, dtype=jnp.int32)[:, None]).astype(jnp.bfloat16)


def place(one_hot_rows, rows):
    return lax.dot_general(
        one_hot_rows, rows, (((1,), (0,)), ((), ())), preferred_element_type=jnp.float32
    ).astype(jnp.bfloat16)


def exchange(rows, expert_count):
    slots, width = rows.shape
    return lax.all_to_all(
        rows.reshape(expert_count, slots // expert_count, width),
        "exp",
        split_axis=0,
        concat_axis=0,
        tiled=True,
    ).reshape(slots, width)


def swap_with(rows, mask):
    total = lax.axis_size("exp")
    return lax.ppermute(rows, "exp", [(i, i ^ mask) for i in range(total)])


def double(rows, mask):
    return jnp.concatenate([rows, swap_with(rows, mask)], axis=0)


def halves(rows):
    half = rows.shape[0] // 2
    return rows[:half], rows[half:]


def halve(rows, mask):
    kept, sent = halves(rows)
    return kept + swap_with(sent, mask)


def outer_masks():
    masks = []
    bit = lax.axis_size("exp") // 2
    while bit > 2:
        masks.append(bit)
        bit //= 2
    return masks


def swap_quarters(rows):
    quarter = rows.shape[0] // 4
    parts = [rows[i * quarter : (i + 1) * quarter] for i in (0, 2, 1, 3)]
    return jnp.concatenate(parts, axis=0)


def block_of(extent, most):
    size = most
    while extent % size:
        size //= 2
    return size


def dot_f32(left, right, left_dim, right_dim):
    return lax.dot_general(
        left, right, (((left_dim,), (right_dim,)), ((), ())), preferred_element_type=jnp.float32
    )


def product_kernel(right_dim, left_ref, right_ref, out_ref):
    out_ref[...] = dot_f32(left_ref[...], right_ref[...], 1, right_dim).astype(out_ref.dtype)


def product(left, column_block, depth, right, transposed):
    height = left.shape[0]
    width = right.shape[0] if transposed else right.shape[1]
    step = block_of(width, 256)
    if transposed:
        right_spec = pl.BlockSpec((step, depth), lambda j: (j, 0))
    else:
        right_spec = pl.BlockSpec((depth, step), lambda j: (0, j))
    return pl.pallas_call(
        functools.partial(product_kernel, 1 if transposed else 0),
        grid=(width // step,),
        in_specs=[pl.BlockSpec((height, depth), lambda j: (0, column_block)), right_spec],
        out_specs=pl.BlockSpec((height, step), lambda j: (0, j)),
        out_shape=jax.ShapeDtypeStruct((height, width), jnp.bfloat16),
        compiler_params=pltpu.CompilerParams(vmem_limit_bytes=VMEM_BYTES),
        cost_estimate=SMALL_COST,
    )(left, right)


def pair_over_grp(part):
    if lax.axis_size("grp") == 2:
        return part, lax.ppermute(part, "grp", [(0, 1), (1, 0)])
    return lax.psum(part, "grp"), jnp.zeros_like(part)


def finish_kernel(
    keep_ref, gate_a, gate_b, grad_a, grad_b, matrix_ref, out_ref, hidden_ref, branch_ref
):
    height, width = hidden_ref.shape

    @pl.when(pl.program_id(0) == 0)
    def _():
        keep = keep_ref[0] > 0
        step = block_of(height, 32)

        @pl.loop(0, height // step)
        def _(i):
            here = pl.ds(pl.multiple_of(i * step, step), step)

            def total(one, two, columns):
                return one[here, columns].astype(jnp.float32) + two[here, columns].astype(
                    jnp.float32
                )

            gate_value = total(gate_a, gate_b, pl.ds(0, width))
            upward = total(gate_a, gate_b, pl.ds(width, width))
            hidden_grads = total(grad_a, grad_b, pl.ds(0, width))
            sigmoid_value = jax.nn.sigmoid(gate_value)
            activated = gate_value * sigmoid_value
            gate_slope = sigmoid_value * (1.0 + gate_value * (1.0 - sigmoid_value))

            def put(ref, columns, value):
                ref[here, columns] = jnp.where(keep, value, 0.0).astype(ref.dtype)

            put(hidden_ref, pl.ds(0, width), activated * upward)
            put(branch_ref, pl.ds(0, width), hidden_grads * upward * gate_slope)
            put(branch_ref, pl.ds(width, width), hidden_grads * activated)

    out_ref[...] = dot_f32(branch_ref[...], matrix_ref[...], 1, 1).astype(out_ref.dtype)


def finish(keep, gate_pair, grad_pair, matrix):
    height, width = grad_pair[0].shape
    features = matrix.shape[0]
    step = block_of(features, 512)
    whole = lambda columns: pl.BlockSpec((height, columns), lambda j: (0, 0))
    shape = lambda columns: jax.ShapeDtypeStruct((height, columns), jnp.bfloat16)
    return pl.pallas_call(
        finish_kernel,
        grid=(features // step,),
        in_specs=[
            pl.BlockSpec(memory_space=pltpu.SMEM),
            whole(2 * width),
            whole(2 * width),
            whole(width),
            whole(width),
            pl.BlockSpec((step, 2 * width), lambda j: (j, 0)),
        ],
        out_specs=[
            pl.BlockSpec((height, step), lambda j: (0, j)),
            whole(width),
            whole(2 * width),
        ],
        out_shape=[shape(features), shape(width), shape(2 * width)],
        compiler_params=pltpu.CompilerParams(vmem_limit_bytes=VMEM_BYTES),
        cost_estimate=SMALL_COST,
    )(keep, *gate_pair, *grad_pair, matrix)


def outer(left, right):
    return lax.dot_general(
        left, right, (((0,), (0,)), ((), ())), preferred_element_type=jnp.float32
    ).astype(jnp.bfloat16)


def local(tokens, d_out, row_expert, w_gate_up, w_down):
    row_count, feature_share = tokens.shape
    hidden_width = w_down.shape[1]
    expert_count = lax.axis_size("exp")
    gate_up_matrix = w_gate_up.reshape(feature_share, 2 * hidden_width)
    down_matrix = w_down.reshape(hidden_width, feature_share)
    cap = 2 * row_count // expert_count
    bounds = (0, cap // 2, cap)

    rank = rank_in_expert(row_expert)
    is_spill = rank >= cap
    busiest = jnp.max(jnp.where(is_spill, row_expert, -1))
    is_busiest = lax.axis_index("exp") == busiest
    spill_hot = one_hot(jnp.where(is_spill, rank - cap, -1), cap)
    chunk_hot = []
    for low, high in zip(bounds, bounds[1:]):
        inside = (rank >= low) & (rank < high)
        slot = row_expert * (high - low) + rank - low
        chunk_hot.append(one_hot(jnp.where(inside, slot, -1), expert_count * (high - low)))

    both = jnp.concatenate([tokens, d_out], axis=1)

    def split(both_in):
        return both_in[:, :feature_share], both_in[:, feature_share:]

    def products(rows_in, rows_block, grads_in, grads_block):
        gate_part = product(rows_in, rows_block, feature_share, gate_up_matrix, False)
        grad_part = product(grads_in, grads_block, feature_share, down_matrix, True)
        return pair_over_grp(gate_part), pair_over_grp(grad_part)

    always = jnp.ones((1,), jnp.int32)
    only_busiest = is_busiest.astype(jnp.int32).reshape(1)

    far = outer_masks()
    spill_both = place(spill_hot, both)
    for mask in far:
        spill_both = double(spill_both, mask)
    spill_rows, spill_grads = split(spill_both)
    sent_0 = place(chunk_hot[0], both)
    spill_rows, spill_grads, sent_0 = lax.optimization_barrier((spill_rows, spill_grads, sent_0))

    arrived_0 = exchange(sent_0, expert_count)
    spill_rows = double(double(spill_rows, 2), 1)
    spill_grads = swap_quarters(double(double(spill_grads, 1), 2))
    sent_1 = place(chunk_hot[1], both)
    arrived_0, spill_rows, spill_grads, sent_1, gate_up_matrix = lax.optimization_barrier(
        (arrived_0, spill_rows, spill_grads, sent_1, gate_up_matrix)
    )

    arrived_1 = exchange(sent_1, expert_count)
    out_s, hidden_s, branch_s = finish(
        only_busiest, *products(spill_rows, 0, spill_grads, 0), gate_up_matrix
    )
    middle = feature_share // 2
    kept_a, sent_a = halves(out_s[:, :middle])
    kept_b, sent_b = halves(swap_quarters(out_s[:, middle:]))
    arrived_0, kept_a, sent_a, kept_b, sent_b = lax.optimization_barrier(
        (arrived_0, kept_a, sent_a, kept_b, sent_b)
    )
    come_a, come_b = swap_with(sent_a, 1), swap_with(sent_b, 2)
    out_0, hidden_0, branch_0 = finish(
        always, *products(arrived_0, 0, arrived_0, 1), gate_up_matrix
    )
    rows_0, grads_0 = split(arrived_0)
    arrived_1, out_0, come_a, come_b = lax.optimization_barrier(
        (arrived_1, out_0, come_a, come_b)
    )

    back_0 = exchange(out_0, expert_count)
    kept_a, sent_a = halves(kept_a + come_a)
    kept_b, sent_b = halves(kept_b + come_b)
    come_a, come_b = swap_with(sent_a, 2), swap_with(sent_b, 1)
    out_1, hidden_1, branch_1 = finish(
        always, *products(arrived_1, 0, arrived_1, 1), gate_up_matrix
    )
    back_0, come_a, come_b, out_1, arrived_1 = lax.optimization_barrier(
        (back_0, come_a, come_b, out_1, arrived_1)
    )
    back_s = jnp.concatenate([kept_a + come_a, kept_b + come_b], axis=1)

    for mask in reversed(far[1:]):
        back_s = halve(back_s, mask)
    rows_1, grads_1 = split(arrived_1)
    back_1 = exchange(out_1, expert_count)

    all_rows = jnp.concatenate([spill_rows, rows_0, rows_1], axis=0)
    all_grads = jnp.concatenate([spill_grads, grads_0, grads_1], axis=0)
    hidden = jnp.concatenate([hidden_s, hidden_0, hidden_1], axis=0)
    branch = jnp.concatenate([branch_s, branch_0, branch_1], axis=0)
    gate_up_grads = with_layout_constraint(outer(all_rows, branch), Layout((0, 1)))
    down_grads = outer(hidden, all_grads).reshape(1, hidden_width, feature_share)
    gate_up_grads = gate_up_grads.reshape(feature_share // 8, 8, 2, hidden_width)
    back_s, gate_up_grads, down_grads = lax.optimization_barrier(
        (back_s, gate_up_grads.transpose(0, 2, 1, 3), down_grads)
    )

    back_s = halve(back_s, far[0])
    gate_up_grads = gate_up_grads.transpose(0, 2, 1, 3).reshape(
        1, feature_share, 2, hidden_width
    )

    pick = jnp.concatenate([spill_hot] + chunk_hot, axis=0)
    returned = jnp.concatenate([back_s, back_0, back_1], axis=0)
    token_grads = lax.dot_general(
        pick, returned, (((0,), (0,)), ((), ())), preferred_element_type=jnp.float32
    ).astype(jnp.bfloat16)
    return (token_grads, gate_up_grads, down_grads)


def solution(mesh):
    return jax.shard_map(
        local,
        mesh=mesh,
        in_specs=(
            P("exp", "grp"),
            P("exp", "grp"),
            P("exp"),
            P("exp", "grp", None, None),
            P("exp", None, "grp"),
        ),
        out_specs=(P("exp", "grp"), P("exp", "grp", None, None), P("exp", None, "grp")),
        check_vma=False,
    )
```

```python
import functools

import jax
import jax.numpy as jnp
from jax import lax
from jax.experimental import pallas as pl
from jax.experimental.layout import Layout, with_layout_constraint
from jax.experimental.pallas import tpu as pltpu
from jax.sharding import PartitionSpec as P

VMEM_BYTES = 48 * 1024 * 1024
SMALL_COST = pl.CostEstimate(flops=1, bytes_accessed=1, transcendentals=0)


def rank_in_expert(row_expert):
    row_count = row_expert.shape[0]
    same = row_expert[:, None] == row_expert[None, :]
    earlier = jnp.arange(row_count)[None, :] < jnp.arange(row_count)[:, None]
    return jnp.sum((same & earlier).astype(jnp.int32), axis=1)


def one_hot(index, total):
    return (index[None, :] == jnp.arange(total, dtype=jnp.int32)[:, None]).astype(jnp.bfloat16)


def place(one_hot_rows, rows):
    return lax.dot_general(
        one_hot_rows, rows, (((1,), (0,)), ((), ())), preferred_element_type=jnp.float32
    ).astype(jnp.bfloat16)


def exchange(rows, expert_count):
    slots, width = rows.shape
    return lax.all_to_all(
        rows.reshape(expert_count, slots // expert_count, width),
        "exp",
        split_axis=0,
        concat_axis=0,
        tiled=True,
    ).reshape(slots, width)


def swap_with(rows, mask):
    total = lax.axis_size("exp")
    return lax.ppermute(rows, "exp", [(i, i ^ mask) for i in range(total)])


def double(rows, mask):
    return jnp.concatenate([rows, swap_with(rows, mask)], axis=0)


def halves(rows):
    half = rows.shape[0] // 2
    return rows[:half], rows[half:]


def halve(rows, mask):
    kept, sent = halves(rows)
    return kept + swap_with(sent, mask)


def outer_masks():
    masks = []
    bit = lax.axis_size("exp") // 2
    while bit > 2:
        masks.append(bit)
        bit //= 2
    return masks


def swap_quarters(rows):
    quarter = rows.shape[0] // 4
    parts = [rows[i * quarter : (i + 1) * quarter] for i in (0, 2, 1, 3)]
    return jnp.concatenate(parts, axis=0)


def block_of(extent, most):
    size = most
    while extent % size:
        size //= 2
    return size


def dot_f32(left, right, left_dim, right_dim):
    return lax.dot_general(
        left, right, (((left_dim,), (right_dim,)), ((), ())), preferred_element_type=jnp.float32
    )


def product_kernel(right_dim, left_ref, right_ref, out_ref):
    out_ref[...] = dot_f32(left_ref[...], right_ref[...], 1, right_dim).astype(out_ref.dtype)


def product(left, column_block, depth, right, transposed):
    height = left.shape[0]
    width = right.shape[0] if transposed else right.shape[1]
    step = block_of(width, 256)
    if transposed:
        right_spec = pl.BlockSpec((step, depth), lambda j: (j, 0))
    else:
        right_spec = pl.BlockSpec((depth, step), lambda j: (0, j))
    return pl.pallas_call(
        functools.partial(product_kernel, 1 if transposed else 0),
        grid=(width // step,),
        in_specs=[pl.BlockSpec((height, depth), lambda j: (0, column_block)), right_spec],
        out_specs=pl.BlockSpec((height, step), lambda j: (0, j)),
        out_shape=jax.ShapeDtypeStruct((height, width), jnp.bfloat16),
        compiler_params=pltpu.CompilerParams(vmem_limit_bytes=VMEM_BYTES),
        cost_estimate=SMALL_COST,
    )(left, right)


def pair_over_grp(part):
    if lax.axis_size("grp") == 2:
        return part, lax.ppermute(part, "grp", [(0, 1), (1, 0)])
    return lax.psum(part, "grp"), jnp.zeros_like(part)


def finish_kernel(
    keep_ref, gate_a, gate_b, grad_a, grad_b, matrix_ref, out_ref, hidden_ref, branch_ref
):
    height, width = hidden_ref.shape

    @pl.when(pl.program_id(0) == 0)
    def _():
        keep = keep_ref[0] > 0
        step = block_of(height, 32)

        @pl.loop(0, height // step)
        def _(i):
            here = pl.ds(pl.multiple_of(i * step, step), step)

            def total(one, two, columns):
                return one[here, columns].astype(jnp.float32) + two[here, columns].astype(
                    jnp.float32
                )

            gate_value = total(gate_a, gate_b, pl.ds(0, width))
            upward = total(gate_a, gate_b, pl.ds(width, width))
            hidden_grads = total(grad_a, grad_b, pl.ds(0, width))
            sigmoid_value = jax.nn.sigmoid(gate_value)
            activated = gate_value * sigmoid_value
            gate_slope = sigmoid_value * (1.0 + gate_value * (1.0 - sigmoid_value))

            def put(ref, columns, value):
                ref[here, columns] = jnp.where(keep, value, 0.0).astype(ref.dtype)

            put(hidden_ref, pl.ds(0, width), activated * upward)
            put(branch_ref, pl.ds(0, width), hidden_grads * upward * gate_slope)
            put(branch_ref, pl.ds(width, width), hidden_grads * activated)

    out_ref[...] = dot_f32(branch_ref[...], matrix_ref[...], 1, 1).astype(out_ref.dtype)


def finish(keep, gate_pair, grad_pair, matrix):
    height, width = grad_pair[0].shape
    features = matrix.shape[0]
    step = block_of(features, 512)
    whole = lambda columns: pl.BlockSpec((height, columns), lambda j: (0, 0))
    shape = lambda columns: jax.ShapeDtypeStruct((height, columns), jnp.bfloat16)
    return pl.pallas_call(
        finish_kernel,
        grid=(features // step,),
        in_specs=[
            pl.BlockSpec(memory_space=pltpu.SMEM),
            whole(2 * width),
            whole(2 * width),
            whole(width),
            whole(width),
            pl.BlockSpec((step, 2 * width), lambda j: (j, 0)),
        ],
        out_specs=[
            pl.BlockSpec((height, step), lambda j: (0, j)),
            whole(width),
            whole(2 * width),
        ],
        out_shape=[shape(features), shape(width), shape(2 * width)],
        compiler_params=pltpu.CompilerParams(vmem_limit_bytes=VMEM_BYTES),
        cost_estimate=SMALL_COST,
    )(keep, *gate_pair, *grad_pair, matrix)


def outer(left, right):
    return lax.dot_general(
        left, right, (((0,), (0,)), ((), ())), preferred_element_type=jnp.float32
    ).astype(jnp.bfloat16)


def local(tokens, d_out, row_expert, w_gate_up, w_down):
    row_count, feature_share = tokens.shape
    hidden_width = w_down.shape[1]
    expert_count = lax.axis_size("exp")
    gate_up_matrix = w_gate_up.reshape(feature_share, 2 * hidden_width)
    down_matrix = w_down.reshape(hidden_width, feature_share)
    cap = 2 * row_count // expert_count
    bounds = (0, cap // 2, cap)

    rank = rank_in_expert(row_expert)
    is_spill = rank >= cap
    busiest = jnp.max(jnp.where(is_spill, row_expert, -1))
    is_busiest = lax.axis_index("exp") == busiest
    spill_hot = one_hot(jnp.where(is_spill, rank - cap, -1), cap)
    chunk_hot = []
    for low, high in zip(bounds, bounds[1:]):
        inside = (rank >= low) & (rank < high)
        slot = row_expert * (high - low) + rank - low
        chunk_hot.append(one_hot(jnp.where(inside, slot, -1), expert_count * (high - low)))

    both = jnp.concatenate([tokens, d_out], axis=1)

    def split(both_in):
        return both_in[:, :feature_share], both_in[:, feature_share:]

    def products(rows_in, rows_block, grads_in, grads_block):
        gate_part = product(rows_in, rows_block, feature_share, gate_up_matrix, False)
        grad_part = product(grads_in, grads_block, feature_share, down_matrix, True)
        return pair_over_grp(gate_part), pair_over_grp(grad_part)

    always = jnp.ones((1,), jnp.int32)
    only_busiest = is_busiest.astype(jnp.int32).reshape(1)

    far = outer_masks()
    spill_both = jnp.concatenate([place(spill_hot, tokens), place(spill_hot, d_out)], axis=1)
    for mask in far:
        spill_both = double(spill_both, mask)
    spill_rows, spill_grads = split(spill_both)
    sent_0 = place(chunk_hot[0], both)
    spill_rows, spill_grads, sent_0 = lax.optimization_barrier((spill_rows, spill_grads, sent_0))

    arrived_0 = exchange(sent_0, expert_count)
    spill_rows = double(double(spill_rows, 2), 1)
    spill_grads = swap_quarters(double(double(spill_grads, 1), 2))
    sent_1 = place(chunk_hot[1], both)
    arrived_0, spill_rows, spill_grads, sent_1, gate_up_matrix = lax.optimization_barrier(
        (arrived_0, spill_rows, spill_grads, sent_1, gate_up_matrix)
    )

    arrived_1 = exchange(sent_1, expert_count)
    out_s, hidden_s, branch_s = finish(
        only_busiest, *products(spill_rows, 0, spill_grads, 0), gate_up_matrix
    )
    middle = feature_share // 2
    kept_a, sent_a = halves(out_s[:, :middle])
    kept_b, sent_b = halves(swap_quarters(out_s[:, middle:]))
    arrived_0, kept_a, sent_a, kept_b, sent_b = lax.optimization_barrier(
        (arrived_0, kept_a, sent_a, kept_b, sent_b)
    )
    come_a, come_b = swap_with(sent_a, 1), swap_with(sent_b, 2)
    out_0, hidden_0, branch_0 = finish(
        always, *products(arrived_0, 0, arrived_0, 1), gate_up_matrix
    )
    rows_0, grads_0 = split(arrived_0)
    arrived_1, out_0, come_a, come_b, rows_0, grads_0 = lax.optimization_barrier(
        (arrived_1, out_0, come_a, come_b, rows_0, grads_0)
    )

    back_0 = exchange(out_0, expert_count)
    kept_a, sent_a = halves(kept_a + come_a)
    kept_b, sent_b = halves(kept_b + come_b)
    come_a, come_b = swap_with(sent_a, 2), swap_with(sent_b, 1)
    out_1, hidden_1, branch_1 = finish(
        always, *products(arrived_1, 0, arrived_1, 1), gate_up_matrix
    )
    back_0, come_a, come_b, out_1, arrived_1 = lax.optimization_barrier(
        (back_0, come_a, come_b, out_1, arrived_1)
    )
    back_s = jnp.concatenate([kept_a + come_a, kept_b + come_b], axis=1)

    for mask in reversed(far[1:]):
        back_s = halve(back_s, mask)
    rows_1, grads_1 = split(arrived_1)
    back_1 = exchange(out_1, expert_count)

    hidden = jnp.concatenate([hidden_s, hidden_0, hidden_1], axis=0)
    all_grads = jnp.concatenate([spill_grads, grads_0, grads_1], axis=0)
    down_grads = outer(hidden, all_grads).reshape(1, hidden_width, feature_share)
    down_grads, spill_rows = lax.optimization_barrier((down_grads, spill_rows))
    all_rows = jnp.concatenate([spill_rows, rows_0, rows_1], axis=0)
    branch = jnp.concatenate([branch_s, branch_0, branch_1], axis=0)
    gate_up_grads = with_layout_constraint(outer(all_rows, branch), Layout((0, 1)))
    gate_up_grads = gate_up_grads.reshape(feature_share // 8, 8, 2, hidden_width)
    back_s, gate_up_grads = lax.optimization_barrier(
        (back_s, gate_up_grads.transpose(0, 2, 1, 3))
    )

    back_s = halve(back_s, far[0])
    gate_up_grads = gate_up_grads.transpose(0, 2, 1, 3).reshape(
        1, feature_share, 2, hidden_width
    )

    pick = jnp.concatenate([spill_hot] + chunk_hot, axis=0)
    returned = jnp.concatenate([back_s, back_0, back_1], axis=0)
    token_grads = lax.dot_general(
        pick, returned, (((0,), (0,)), ((), ())), preferred_element_type=jnp.float32
    ).astype(jnp.bfloat16)
    return (token_grads, gate_up_grads, down_grads)


def solution(mesh):
    return jax.shard_map(
        local,
        mesh=mesh,
        in_specs=(
            P("exp", "grp"),
            P("exp", "grp"),
            P("exp"),
            P("exp", "grp", None, None),
            P("exp", None, "grp"),
        ),
        out_specs=(P("exp", "grp"), P("exp", "grp", None, None), P("exp", None, "grp")),
        check_vma=False,
    )
```

```python
import functools

import jax
import jax.numpy as jnp
from jax import lax
from jax.experimental import pallas as pl
from jax.experimental.layout import Layout, with_layout_constraint
from jax.experimental.pallas import tpu as pltpu
from jax.sharding import PartitionSpec as P

VMEM_BYTES = 48 * 1024 * 1024
SMALL_COST = pl.CostEstimate(flops=1, bytes_accessed=1, transcendentals=0)


def rank_in_expert(row_expert):
    row_count = row_expert.shape[0]
    same = row_expert[:, None] == row_expert[None, :]
    earlier = jnp.arange(row_count)[None, :] < jnp.arange(row_count)[:, None]
    return jnp.sum((same & earlier).astype(jnp.int32), axis=1)


def one_hot(index, total):
    return (index[None, :] == jnp.arange(total, dtype=jnp.int32)[:, None]).astype(jnp.bfloat16)


def place(one_hot_rows, rows):
    return lax.dot_general(
        one_hot_rows, rows, (((1,), (0,)), ((), ())), preferred_element_type=jnp.float32
    ).astype(jnp.bfloat16)


def exchange(rows, expert_count):
    slots, width = rows.shape
    return lax.all_to_all(
        rows.reshape(expert_count, slots // expert_count, width),
        "exp",
        split_axis=0,
        concat_axis=0,
        tiled=True,
    ).reshape(slots, width)


def swap_with(rows, mask):
    total = lax.axis_size("exp")
    return lax.ppermute(rows, "exp", [(i, i ^ mask) for i in range(total)])


def double(rows, mask):
    return jnp.concatenate([rows, swap_with(rows, mask)], axis=0)


def halves(rows):
    half = rows.shape[0] // 2
    return rows[:half], rows[half:]


def halve(rows, mask):
    kept, sent = halves(rows)
    return kept + swap_with(sent, mask)


def outer_masks():
    masks = []
    bit = lax.axis_size("exp") // 2
    while bit > 2:
        masks.append(bit)
        bit //= 2
    return masks


def swap_quarters(rows):
    quarter = rows.shape[0] // 4
    parts = [rows[i * quarter : (i + 1) * quarter] for i in (0, 2, 1, 3)]
    return jnp.concatenate(parts, axis=0)


def block_of(extent, most):
    size = most
    while extent % size:
        size //= 2
    return size


def dot_f32(left, right, left_dim, right_dim):
    return lax.dot_general(
        left, right, (((left_dim,), (right_dim,)), ((), ())), preferred_element_type=jnp.float32
    )


def product_kernel(right_dim, left_ref, right_ref, out_ref):
    out_ref[...] = dot_f32(left_ref[...], right_ref[...], 1, right_dim).astype(out_ref.dtype)


def product(left, column_block, depth, right, transposed):
    height = left.shape[0]
    width = right.shape[0] if transposed else right.shape[1]
    step = block_of(width, 256)
    if transposed:
        right_spec = pl.BlockSpec((step, depth), lambda j: (j, 0))
    else:
        right_spec = pl.BlockSpec((depth, step), lambda j: (0, j))
    return pl.pallas_call(
        functools.partial(product_kernel, 1 if transposed else 0),
        grid=(width // step,),
        in_specs=[pl.BlockSpec((height, depth), lambda j: (0, column_block)), right_spec],
        out_specs=pl.BlockSpec((height, step), lambda j: (0, j)),
        out_shape=jax.ShapeDtypeStruct((height, width), jnp.bfloat16),
        compiler_params=pltpu.CompilerParams(vmem_limit_bytes=VMEM_BYTES),
        cost_estimate=SMALL_COST,
    )(left, right)


def pair_over_grp(part):
    if lax.axis_size("grp") == 2:
        return part, lax.ppermute(part, "grp", [(0, 1), (1, 0)])
    return lax.psum(part, "grp"), jnp.zeros_like(part)


def finish_kernel(
    keep_ref, gate_a, gate_b, grad_a, grad_b, matrix_ref, out_ref, hidden_ref, branch_ref
):
    height, width = hidden_ref.shape

    @pl.when(pl.program_id(0) == 0)
    def _():
        keep = keep_ref[0] > 0
        step = block_of(height, 32)

        @pl.loop(0, height // step)
        def _(i):
            here = pl.ds(pl.multiple_of(i * step, step), step)

            def total(one, two, columns):
                return one[here, columns].astype(jnp.float32) + two[here, columns].astype(
                    jnp.float32
                )

            gate_value = total(gate_a, gate_b, pl.ds(0, width))
            upward = total(gate_a, gate_b, pl.ds(width, width))
            hidden_grads = total(grad_a, grad_b, pl.ds(0, width))
            sigmoid_value = jax.nn.sigmoid(gate_value)
            activated = gate_value * sigmoid_value
            gate_slope = sigmoid_value * (1.0 + gate_value * (1.0 - sigmoid_value))

            def put(ref, columns, value):
                ref[here, columns] = jnp.where(keep, value, 0.0).astype(ref.dtype)

            put(hidden_ref, pl.ds(0, width), activated * upward)
            put(branch_ref, pl.ds(0, width), hidden_grads * upward * gate_slope)
            put(branch_ref, pl.ds(width, width), hidden_grads * activated)

    out_ref[...] = dot_f32(branch_ref[...], matrix_ref[...], 1, 1).astype(out_ref.dtype)


def finish(keep, gate_pair, grad_pair, matrix):
    height, width = grad_pair[0].shape
    features = matrix.shape[0]
    step = block_of(features, 512)
    whole = lambda columns: pl.BlockSpec((height, columns), lambda j: (0, 0))
    shape = lambda columns: jax.ShapeDtypeStruct((height, columns), jnp.bfloat16)
    return pl.pallas_call(
        finish_kernel,
        grid=(features // step,),
        in_specs=[
            pl.BlockSpec(memory_space=pltpu.SMEM),
            whole(2 * width),
            whole(2 * width),
            whole(width),
            whole(width),
            pl.BlockSpec((step, 2 * width), lambda j: (j, 0)),
        ],
        out_specs=[
            pl.BlockSpec((height, step), lambda j: (0, j)),
            whole(width),
            whole(2 * width),
        ],
        out_shape=[shape(features), shape(width), shape(2 * width)],
        compiler_params=pltpu.CompilerParams(vmem_limit_bytes=VMEM_BYTES),
        cost_estimate=SMALL_COST,
    )(keep, *gate_pair, *grad_pair, matrix)


def outer_kernel(count, *refs):
    out_ref = refs[-1]
    total = dot_f32(refs[0][...], refs[count][...], 0, 0)
    for left_ref, right_ref in zip(refs[1:count], refs[count + 1 : -1]):
        total += dot_f32(left_ref[...], right_ref[...], 0, 0)
    out_ref[...] = total.astype(out_ref.dtype)


def outer_of_pieces(lefts, rights, shares, share):
    width = lefts[0].shape[1]
    step = block_of(share, 512)
    steps = share // step
    rows = sum(left.shape[0] for left in lefts)

    def columns(part):
        return lambda j: (0, part * steps + j)

    return pl.pallas_call(
        functools.partial(outer_kernel, len(lefts)),
        grid=(steps,),
        in_specs=[pl.BlockSpec(left.shape, lambda j: (0, 0)) for left in lefts]
        + [
            pl.BlockSpec((right.shape[0], step), columns(part))
            for right, part in zip(rights, shares)
        ],
        out_specs=pl.BlockSpec((width, step), lambda j: (0, j)),
        out_shape=jax.ShapeDtypeStruct((width, share), jnp.bfloat16),
        compiler_params=pltpu.CompilerParams(vmem_limit_bytes=VMEM_BYTES // 2),
        cost_estimate=pl.CostEstimate(
            flops=2 * rows * width * share,
            bytes_accessed=2 * (rows * (width + share) + width * share),
            transcendentals=0,
        ),
    )(*lefts, *rights)


def outer(left, right):
    return lax.dot_general(
        left, right, (((0,), (0,)), ((), ())), preferred_element_type=jnp.float32
    ).astype(jnp.bfloat16)


def local(tokens, d_out, row_expert, w_gate_up, w_down):
    row_count, feature_share = tokens.shape
    hidden_width = w_down.shape[1]
    expert_count = lax.axis_size("exp")
    gate_up_matrix = w_gate_up.reshape(feature_share, 2 * hidden_width)
    down_matrix = w_down.reshape(hidden_width, feature_share)
    cap = 2 * row_count // expert_count
    bounds = (0, cap // 2, cap)

    rank = rank_in_expert(row_expert)
    is_spill = rank >= cap
    busiest = jnp.max(jnp.where(is_spill, row_expert, -1))
    is_busiest = lax.axis_index("exp") == busiest
    spill_hot = one_hot(jnp.where(is_spill, rank - cap, -1), cap)
    chunk_hot = []
    for low, high in zip(bounds, bounds[1:]):
        inside = (rank >= low) & (rank < high)
        slot = row_expert * (high - low) + rank - low
        chunk_hot.append(one_hot(jnp.where(inside, slot, -1), expert_count * (high - low)))

    both = jnp.concatenate([tokens, d_out], axis=1)

    def split(both_in):
        return both_in[:, :feature_share], both_in[:, feature_share:]

    def products(rows_in, rows_block, grads_in, grads_block):
        gate_part = product(rows_in, rows_block, feature_share, gate_up_matrix, False)
        grad_part = product(grads_in, grads_block, feature_share, down_matrix, True)
        return pair_over_grp(gate_part), pair_over_grp(grad_part)

    always = jnp.ones((1,), jnp.int32)
    only_busiest = is_busiest.astype(jnp.int32).reshape(1)

    far = outer_masks()
    spill_both = place(spill_hot, both)
    for mask in far:
        spill_both = double(spill_both, mask)
    spill_rows, spill_grads = split(spill_both)
    sent_0 = place(chunk_hot[0], both)
    spill_rows, spill_grads, sent_0 = lax.optimization_barrier((spill_rows, spill_grads, sent_0))

    arrived_0 = exchange(sent_0, expert_count)
    spill_rows = double(double(spill_rows, 2), 1)
    spill_grads = swap_quarters(double(double(spill_grads, 1), 2))
    sent_1 = place(chunk_hot[1], both)
    arrived_0, spill_rows, spill_grads, sent_1, gate_up_matrix = lax.optimization_barrier(
        (arrived_0, spill_rows, spill_grads, sent_1, gate_up_matrix)
    )

    arrived_1 = exchange(sent_1, expert_count)
    out_s, hidden_s, branch_s = finish(
        only_busiest, *products(spill_rows, 0, spill_grads, 0), gate_up_matrix
    )
    middle = feature_share // 2
    kept_a, sent_a = halves(out_s[:, :middle])
    kept_b, sent_b = halves(swap_quarters(out_s[:, middle:]))
    arrived_0, kept_a, sent_a, kept_b, sent_b = lax.optimization_barrier(
        (arrived_0, kept_a, sent_a, kept_b, sent_b)
    )
    come_a, come_b = swap_with(sent_a, 1), swap_with(sent_b, 2)
    out_0, hidden_0, branch_0 = finish(
        always, *products(arrived_0, 0, arrived_0, 1), gate_up_matrix
    )
    rows_0, _ = split(arrived_0)
    arrived_1, out_0, rows_0 = lax.optimization_barrier((arrived_1, out_0, rows_0))

    back_0 = exchange(out_0, expert_count)
    come_a, come_b, gate_pair, grad_pair = lax.optimization_barrier(
        (come_a, come_b, *products(arrived_1, 0, arrived_1, 1))
    )
    kept_a, sent_a = halves(kept_a + come_a)
    kept_b, sent_b = halves(kept_b + come_b)
    come_a, come_b = swap_with(sent_a, 2), swap_with(sent_b, 1)
    out_1, hidden_1, branch_1 = finish(always, gate_pair, grad_pair, gate_up_matrix)
    back_0, come_a, come_b, out_1, arrived_1 = lax.optimization_barrier(
        (back_0, come_a, come_b, out_1, arrived_1)
    )
    back_s = jnp.concatenate([kept_a + come_a, kept_b + come_b], axis=1)

    for mask in reversed(far[1:]):
        back_s = halve(back_s, mask)
    rows_1, _ = split(arrived_1)
    back_1 = exchange(out_1, expert_count)

    all_rows = jnp.concatenate([spill_rows, rows_0, rows_1], axis=0)
    branch = jnp.concatenate([branch_s, branch_0, branch_1], axis=0)
    gate_up_grads = with_layout_constraint(outer(all_rows, branch), Layout((0, 1)))
    down_grads = outer_of_pieces(
        (hidden_s, hidden_0, hidden_1),
        (spill_grads, arrived_0, arrived_1),
        (0, 1, 1),
        feature_share,
    ).reshape(1, hidden_width, feature_share)
    gate_up_grads = gate_up_grads.reshape(feature_share // 8, 8, 2, hidden_width)
    back_s, gate_up_grads, down_grads = lax.optimization_barrier(
        (back_s, gate_up_grads.transpose(0, 2, 1, 3), down_grads)
    )

    back_s = halve(back_s, far[0])
    gate_up_grads = gate_up_grads.transpose(0, 2, 1, 3).reshape(
        1, feature_share, 2, hidden_width
    )

    pick = jnp.concatenate([spill_hot] + chunk_hot, axis=0)
    returned = jnp.concatenate([back_s, back_0, back_1], axis=0)
    token_grads = lax.dot_general(
        pick, returned, (((0,), (0,)), ((), ())), preferred_element_type=jnp.float32
    ).astype(jnp.bfloat16)
    return (token_grads, gate_up_grads, down_grads)


def solution(mesh):
    return jax.shard_map(
        local,
        mesh=mesh,
        in_specs=(
            P("exp", "grp"),
            P("exp", "grp"),
            P("exp"),
            P("exp", "grp", None, None),
            P("exp", None, "grp"),
        ),
        out_specs=(P("exp", "grp"), P("exp", "grp", None, None), P("exp", None, "grp")),
        check_vma=False,
    )
```

```python
import functools

import jax
import jax.numpy as jnp
from jax import lax
from jax.experimental import pallas as pl
from jax.experimental.layout import Layout, with_layout_constraint
from jax.experimental.pallas import tpu as pltpu
from jax.sharding import PartitionSpec as P

VMEM_BYTES = 48 * 1024 * 1024
SMALL_COST = pl.CostEstimate(flops=1, bytes_accessed=1, transcendentals=0)


def rank_in_expert(row_expert):
    row_count = row_expert.shape[0]
    same = row_expert[:, None] == row_expert[None, :]
    earlier = jnp.arange(row_count)[None, :] < jnp.arange(row_count)[:, None]
    return jnp.sum((same & earlier).astype(jnp.int32), axis=1)


def one_hot(index, total):
    return (index[None, :] == jnp.arange(total, dtype=jnp.int32)[:, None]).astype(jnp.bfloat16)


def place(one_hot_rows, rows):
    return lax.dot_general(
        one_hot_rows, rows, (((1,), (0,)), ((), ())), preferred_element_type=jnp.float32
    ).astype(jnp.bfloat16)


def exchange(rows, expert_count):
    slots, width = rows.shape
    return lax.all_to_all(
        rows.reshape(expert_count, slots // expert_count, width),
        "exp",
        split_axis=0,
        concat_axis=0,
        tiled=True,
    ).reshape(slots, width)


def swap_with(rows, mask):
    total = lax.axis_size("exp")
    return lax.ppermute(rows, "exp", [(i, i ^ mask) for i in range(total)])


def double(rows, mask):
    return jnp.concatenate([rows, swap_with(rows, mask)], axis=0)


def halves(rows):
    half = rows.shape[0] // 2
    return rows[:half], rows[half:]


def halve(rows, mask):
    kept, sent = halves(rows)
    return kept + swap_with(sent, mask)


def outer_masks():
    masks = []
    bit = lax.axis_size("exp") // 2
    while bit > 2:
        masks.append(bit)
        bit //= 2
    return masks


def swap_quarters(rows):
    quarter = rows.shape[0] // 4
    parts = [rows[i * quarter : (i + 1) * quarter] for i in (0, 2, 1, 3)]
    return jnp.concatenate(parts, axis=0)


def block_of(extent, most):
    size = most
    while extent % size:
        size //= 2
    return size


def dot_f32(left, right, left_dim, right_dim):
    return lax.dot_general(
        left, right, (((left_dim,), (right_dim,)), ((), ())), preferred_element_type=jnp.float32
    )


def product_kernel(right_dim, left_ref, right_ref, out_ref):
    out_ref[...] = dot_f32(left_ref[...], right_ref[...], 1, right_dim).astype(out_ref.dtype)


def product(left, column_block, depth, right, transposed):
    height = left.shape[0]
    width = right.shape[0] if transposed else right.shape[1]
    step = block_of(width, 256)
    if transposed:
        right_spec = pl.BlockSpec((step, depth), lambda j: (j, 0))
    else:
        right_spec = pl.BlockSpec((depth, step), lambda j: (0, j))
    return pl.pallas_call(
        functools.partial(product_kernel, 1 if transposed else 0),
        grid=(width // step,),
        in_specs=[pl.BlockSpec((height, depth), lambda j: (0, column_block)), right_spec],
        out_specs=pl.BlockSpec((height, step), lambda j: (0, j)),
        out_shape=jax.ShapeDtypeStruct((height, width), jnp.bfloat16),
        compiler_params=pltpu.CompilerParams(vmem_limit_bytes=VMEM_BYTES),
        cost_estimate=SMALL_COST,
    )(left, right)


def pair_over_grp(part):
    if lax.axis_size("grp") == 2:
        return part, lax.ppermute(part, "grp", [(0, 1), (1, 0)])
    return lax.psum(part, "grp"), jnp.zeros_like(part)


def finish_kernel(
    keep_ref, gate_a, gate_b, grad_a, grad_b, matrix_ref, out_ref, hidden_ref, branch_ref
):
    height, width = hidden_ref.shape

    @pl.when(pl.program_id(0) == 0)
    def _():
        keep = keep_ref[0] > 0
        step = block_of(height, 32)

        @pl.loop(0, height // step)
        def _(i):
            here = pl.ds(pl.multiple_of(i * step, step), step)

            def total(one, two, columns):
                return one[here, columns].astype(jnp.float32) + two[here, columns].astype(
                    jnp.float32
                )

            gate_value = total(gate_a, gate_b, pl.ds(0, width))
            upward = total(gate_a, gate_b, pl.ds(width, width))
            hidden_grads = total(grad_a, grad_b, pl.ds(0, width))
            sigmoid_value = jax.nn.sigmoid(gate_value)
            activated = gate_value * sigmoid_value
            gate_slope = sigmoid_value * (1.0 + gate_value * (1.0 - sigmoid_value))

            def put(ref, columns, value):
                ref[here, columns] = jnp.where(keep, value, 0.0).astype(ref.dtype)

            put(hidden_ref, pl.ds(0, width), activated * upward)
            put(branch_ref, pl.ds(0, width), hidden_grads * upward * gate_slope)
            put(branch_ref, pl.ds(width, width), hidden_grads * activated)

    out_ref[...] = dot_f32(branch_ref[...], matrix_ref[...], 1, 1).astype(out_ref.dtype)


def finish(keep, gate_pair, grad_pair, matrix):
    height, width = grad_pair[0].shape
    features = matrix.shape[0]
    step = block_of(features, 512)
    whole = lambda columns: pl.BlockSpec((height, columns), lambda j: (0, 0))
    shape = lambda columns: jax.ShapeDtypeStruct((height, columns), jnp.bfloat16)
    return pl.pallas_call(
        finish_kernel,
        grid=(features // step,),
        in_specs=[
            pl.BlockSpec(memory_space=pltpu.SMEM),
            whole(2 * width),
            whole(2 * width),
            whole(width),
            whole(width),
            pl.BlockSpec((step, 2 * width), lambda j: (j, 0)),
        ],
        out_specs=[
            pl.BlockSpec((height, step), lambda j: (0, j)),
            whole(width),
            whole(2 * width),
        ],
        out_shape=[shape(features), shape(width), shape(2 * width)],
        compiler_params=pltpu.CompilerParams(vmem_limit_bytes=VMEM_BYTES),
        cost_estimate=SMALL_COST,
    )(keep, *gate_pair, *grad_pair, matrix)


def outer_kernel(count, *refs):
    out_ref = refs[-1]
    total = dot_f32(refs[0][...], refs[count][...], 0, 0)
    for left_ref, right_ref in zip(refs[1:count], refs[count + 1 : -1]):
        total += dot_f32(left_ref[...], right_ref[...], 0, 0)
    out_ref[...] = total.astype(out_ref.dtype)


def outer_of_pieces(lefts, rights, shares, share):
    width = lefts[0].shape[1]
    step = block_of(share, 512)
    steps = share // step
    rows = sum(left.shape[0] for left in lefts)

    def columns(part):
        return lambda j: (0, part * steps + j)

    return pl.pallas_call(
        functools.partial(outer_kernel, len(lefts)),
        grid=(steps,),
        in_specs=[pl.BlockSpec(left.shape, lambda j: (0, 0)) for left in lefts]
        + [
            pl.BlockSpec((right.shape[0], step), columns(part))
            for right, part in zip(rights, shares)
        ],
        out_specs=pl.BlockSpec((width, step), lambda j: (0, j)),
        out_shape=jax.ShapeDtypeStruct((width, share), jnp.bfloat16),
        compiler_params=pltpu.CompilerParams(vmem_limit_bytes=VMEM_BYTES // 2),
        cost_estimate=pl.CostEstimate(
            flops=2 * rows * width * share,
            bytes_accessed=2 * (rows * (width + share) + width * share),
            transcendentals=0,
        ),
    )(*lefts, *rights)


def outer(left, right):
    return lax.dot_general(
        left, right, (((0,), (0,)), ((), ())), preferred_element_type=jnp.float32
    ).astype(jnp.bfloat16)


def local(tokens, d_out, row_expert, w_gate_up, w_down):
    row_count, feature_share = tokens.shape
    hidden_width = w_down.shape[1]
    expert_count = lax.axis_size("exp")
    gate_up_matrix = w_gate_up.reshape(feature_share, 2 * hidden_width)
    down_matrix = w_down.reshape(hidden_width, feature_share)
    cap = 2 * row_count // expert_count
    bounds = (0, cap // 2, cap)

    rank = rank_in_expert(row_expert)
    is_spill = rank >= cap
    busiest = jnp.max(jnp.where(is_spill, row_expert, -1))
    is_busiest = lax.axis_index("exp") == busiest
    spill_hot = one_hot(jnp.where(is_spill, rank - cap, -1), cap)
    chunk_hot = []
    for low, high in zip(bounds, bounds[1:]):
        inside = (rank >= low) & (rank < high)
        slot = row_expert * (high - low) + rank - low
        chunk_hot.append(one_hot(jnp.where(inside, slot, -1), expert_count * (high - low)))

    both = jnp.concatenate([tokens, d_out], axis=1)

    def split(both_in):
        return both_in[:, :feature_share], both_in[:, feature_share:]

    def products(rows_in, rows_block, grads_in, grads_block):
        gate_part = product(rows_in, rows_block, feature_share, gate_up_matrix, False)
        grad_part = product(grads_in, grads_block, feature_share, down_matrix, True)
        return pair_over_grp(gate_part), pair_over_grp(grad_part)

    always = jnp.ones((1,), jnp.int32)
    only_busiest = is_busiest.astype(jnp.int32).reshape(1)

    far = outer_masks()
    spill_both = place(spill_hot, both)
    for mask in far:
        spill_both = double(spill_both, mask)
    spill_rows, spill_grads = split(spill_both)
    sent_0 = place(chunk_hot[0], both)
    spill_rows, spill_grads, sent_0 = lax.optimization_barrier((spill_rows, spill_grads, sent_0))

    arrived_0 = exchange(sent_0, expert_count)
    spill_rows = double(double(spill_rows, 2), 1)
    spill_grads = swap_quarters(double(double(spill_grads, 1), 2))
    sent_1 = place(chunk_hot[1], both)
    arrived_0, spill_rows, spill_grads, sent_1, gate_up_matrix = lax.optimization_barrier(
        (arrived_0, spill_rows, spill_grads, sent_1, gate_up_matrix)
    )

    arrived_1 = exchange(sent_1, expert_count)
    out_s, hidden_s, branch_s = finish(
        only_busiest, *products(spill_rows, 0, spill_grads, 0), gate_up_matrix
    )
    middle = feature_share // 2
    kept_a, sent_a = halves(out_s[:, :middle])
    kept_b, sent_b = halves(swap_quarters(out_s[:, middle:]))
    arrived_0, kept_a, sent_a, kept_b, sent_b = lax.optimization_barrier(
        (arrived_0, kept_a, sent_a, kept_b, sent_b)
    )
    come_a, come_b = swap_with(sent_a, 1), swap_with(sent_b, 2)
    out_0, hidden_0, branch_0 = finish(
        always, *products(arrived_0, 0, arrived_0, 1), gate_up_matrix
    )
    rows_0, _ = split(arrived_0)
    arrived_1, out_0, come_a, come_b, rows_0 = lax.optimization_barrier(
        (arrived_1, out_0, come_a, come_b, rows_0)
    )

    back_0 = exchange(out_0, expert_count)
    kept_a, sent_a = halves(kept_a + come_a)
    kept_b, sent_b = halves(kept_b + come_b)
    come_a, come_b = swap_with(sent_a, 2), swap_with(sent_b, 1)
    out_1, hidden_1, branch_1 = finish(
        always, *products(arrived_1, 0, arrived_1, 1), gate_up_matrix
    )
    back_0, come_a, come_b, out_1, arrived_1 = lax.optimization_barrier(
        (back_0, come_a, come_b, out_1, arrived_1)
    )
    back_s = jnp.concatenate([kept_a + come_a, kept_b + come_b], axis=1)

    for mask in reversed(far[1:]):
        back_s = halve(back_s, mask)
    rows_1, _ = split(arrived_1)
    back_1 = exchange(out_1, expert_count)

    all_rows = jnp.concatenate([spill_rows, rows_0, rows_1], axis=0)
    branch = jnp.concatenate([branch_s, branch_0, branch_1], axis=0)
    gate_up_grads = with_layout_constraint(outer(all_rows, branch), Layout((0, 1)))
    down_grads = outer_of_pieces(
        (hidden_s, hidden_0, hidden_1),
        (spill_grads, arrived_0, arrived_1),
        (0, 1, 1),
        feature_share,
    ).reshape(1, hidden_width, feature_share)
    gate_up_grads = gate_up_grads.reshape(feature_share // 8, 8, 2, hidden_width)
    back_s, gate_up_grads, down_grads = lax.optimization_barrier(
        (back_s, gate_up_grads.transpose(0, 2, 1, 3), down_grads)
    )

    back_s = halve(back_s, far[0])
    gate_up_grads = gate_up_grads.transpose(0, 2, 1, 3).reshape(
        1, feature_share, 2, hidden_width
    )

    pick = jnp.concatenate([spill_hot] + chunk_hot, axis=0)
    returned = jnp.concatenate([back_s, back_0, back_1], axis=0)
    token_grads = lax.dot_general(
        pick, returned, (((0,), (0,)), ((), ())), preferred_element_type=jnp.float32
    ).astype(jnp.bfloat16)
    return (token_grads, gate_up_grads, down_grads)


def solution(mesh):
    return jax.shard_map(
        local,
        mesh=mesh,
        in_specs=(
            P("exp", "grp"),
            P("exp", "grp"),
            P("exp"),
            P("exp", "grp", None, None),
            P("exp", None, "grp"),
        ),
        out_specs=(P("exp", "grp"), P("exp", "grp", None, None), P("exp", None, "grp")),
        check_vma=False,
    )
```

```python
import functools

import jax
import jax.numpy as jnp
from jax import lax
from jax.experimental import pallas as pl
from jax.experimental.layout import Layout, with_layout_constraint
from jax.experimental.pallas import tpu as pltpu
from jax.sharding import PartitionSpec as P

VMEM_BYTES = 48 * 1024 * 1024
SMALL_COST = pl.CostEstimate(flops=1, bytes_accessed=1, transcendentals=0)


def rank_in_expert(row_expert):
    row_count = row_expert.shape[0]
    same = row_expert[:, None] == row_expert[None, :]
    earlier = jnp.arange(row_count)[None, :] < jnp.arange(row_count)[:, None]
    return jnp.sum((same & earlier).astype(jnp.int32), axis=1)


def one_hot(index, total):
    return (index[None, :] == jnp.arange(total, dtype=jnp.int32)[:, None]).astype(jnp.bfloat16)


def place(one_hot_rows, rows):
    return lax.dot_general(
        one_hot_rows, rows, (((1,), (0,)), ((), ())), preferred_element_type=jnp.float32
    ).astype(jnp.bfloat16)


def exchange(rows, expert_count):
    slots, width = rows.shape
    return lax.all_to_all(
        rows.reshape(expert_count, slots // expert_count, width),
        "exp",
        split_axis=0,
        concat_axis=0,
        tiled=True,
    ).reshape(slots, width)


def swap_with(rows, mask):
    total = lax.axis_size("exp")
    return lax.ppermute(rows, "exp", [(i, i ^ mask) for i in range(total)])


def double(rows, mask):
    return jnp.concatenate([rows, swap_with(rows, mask)], axis=0)


def halves(rows):
    half = rows.shape[0] // 2
    return rows[:half], rows[half:]


def halve(rows, mask):
    kept, sent = halves(rows)
    return kept + swap_with(sent, mask)


def outer_masks():
    masks = []
    bit = lax.axis_size("exp") // 2
    while bit > 2:
        masks.append(bit)
        bit //= 2
    return masks


def swap_quarters(rows):
    quarter = rows.shape[0] // 4
    parts = [rows[i * quarter : (i + 1) * quarter] for i in (0, 2, 1, 3)]
    return jnp.concatenate(parts, axis=0)


def block_of(extent, most):
    size = most
    while extent % size:
        size //= 2
    return size


def dot_f32(left, right, left_dim, right_dim):
    return lax.dot_general(
        left, right, (((left_dim,), (right_dim,)), ((), ())), preferred_element_type=jnp.float32
    )


def product_kernel(right_dim, steps, left_ref, right_ref, *out_refs):
    for piece, out_ref in enumerate(out_refs):

        @pl.when(pl.program_id(0) // steps == piece)
        def _():
            out_ref[...] = dot_f32(left_ref[...], right_ref[...], 1, right_dim).astype(
                out_ref.dtype
            )


def product(left, column_block, depth, right, transposed, pieces):
    height = left.shape[0]
    width = right.shape[0] if transposed else right.shape[1]
    share = width // pieces
    step = block_of(share, 256)
    steps = share // step
    if transposed:
        right_spec = pl.BlockSpec((step, depth), lambda j: (j, 0))
    else:
        right_spec = pl.BlockSpec((depth, step), lambda j: (0, j))

    def place_of(piece):
        return lambda j: (0, jnp.clip(j - piece * steps, 0, steps - 1))

    return pl.pallas_call(
        functools.partial(product_kernel, 1 if transposed else 0, steps),
        grid=(width // step,),
        in_specs=[pl.BlockSpec((height, depth), lambda j: (0, column_block)), right_spec],
        out_specs=[pl.BlockSpec((height, step), place_of(piece)) for piece in range(pieces)],
        out_shape=[jax.ShapeDtypeStruct((height, share), jnp.bfloat16)] * pieces,
        compiler_params=pltpu.CompilerParams(vmem_limit_bytes=VMEM_BYTES),
        cost_estimate=SMALL_COST,
    )(left, right)


def pair_over_grp(part):
    if lax.axis_size("grp") == 2:
        return part, lax.ppermute(part, "grp", [(0, 1), (1, 0)])
    return lax.psum(part, "grp"), jnp.zeros_like(part)


def finish_kernel(
    keep_ref,
    gate_a,
    gate_b,
    up_a,
    up_b,
    grad_a,
    grad_b,
    matrix_ref,
    out_ref,
    hidden_ref,
    branch_ref,
):
    height, width = hidden_ref.shape

    @pl.when(pl.program_id(0) == 0)
    def _():
        keep = keep_ref[0] > 0
        step = block_of(height, 32)

        @pl.loop(0, height // step)
        def _(i):
            here = pl.ds(pl.multiple_of(i * step, step), step)

            def total(one, two):
                return one[here, :].astype(jnp.float32) + two[here, :].astype(jnp.float32)

            gate_value = total(gate_a, gate_b)
            upward = total(up_a, up_b)
            hidden_grads = total(grad_a, grad_b)
            sigmoid_value = jax.nn.sigmoid(gate_value)
            activated = gate_value * sigmoid_value
            gate_slope = sigmoid_value * (1.0 + gate_value * (1.0 - sigmoid_value))

            def put(ref, columns, value):
                ref[here, columns] = jnp.where(keep, value, 0.0).astype(ref.dtype)

            put(hidden_ref, pl.ds(0, width), activated * upward)
            put(branch_ref, pl.ds(0, width), hidden_grads * upward * gate_slope)
            put(branch_ref, pl.ds(width, width), hidden_grads * activated)

    out_ref[...] = dot_f32(branch_ref[...], matrix_ref[...], 1, 1).astype(out_ref.dtype)


def finish(keep, gate_pair, up_pair, grad_pair, matrix):
    height, width = grad_pair[0].shape
    features = matrix.shape[0]
    step = block_of(features, 512)
    whole = lambda columns: pl.BlockSpec((height, columns), lambda j: (0, 0))
    shape = lambda columns: jax.ShapeDtypeStruct((height, columns), jnp.bfloat16)
    return pl.pallas_call(
        finish_kernel,
        grid=(features // step,),
        in_specs=[
            pl.BlockSpec(memory_space=pltpu.SMEM),
        ]
        + [whole(width)] * 6
        + [
            pl.BlockSpec((step, 2 * width), lambda j: (j, 0)),
        ],
        out_specs=[
            pl.BlockSpec((height, step), lambda j: (0, j)),
            whole(width),
            whole(2 * width),
        ],
        out_shape=[shape(features), shape(width), shape(2 * width)],
        compiler_params=pltpu.CompilerParams(vmem_limit_bytes=VMEM_BYTES),
        cost_estimate=SMALL_COST,
    )(keep, *gate_pair, *up_pair, *grad_pair, matrix)


def outer_kernel(count, *refs):
    out_ref = refs[-1]
    total = dot_f32(refs[0][...], refs[count][...], 0, 0)
    for left_ref, right_ref in zip(refs[1:count], refs[count + 1 : -1]):
        total += dot_f32(left_ref[...], right_ref[...], 0, 0)
    out_ref[...] = total.astype(out_ref.dtype)


def outer_of_pieces(lefts, rights, shares, share):
    width = lefts[0].shape[1]
    step = block_of(share, 512)
    steps = share // step
    rows = sum(left.shape[0] for left in lefts)

    def columns(part):
        return lambda j: (0, part * steps + j)

    return pl.pallas_call(
        functools.partial(outer_kernel, len(lefts)),
        grid=(steps,),
        in_specs=[pl.BlockSpec(left.shape, lambda j: (0, 0)) for left in lefts]
        + [
            pl.BlockSpec((right.shape[0], step), columns(part))
            for right, part in zip(rights, shares)
        ],
        out_specs=pl.BlockSpec((width, step), lambda j: (0, j)),
        out_shape=jax.ShapeDtypeStruct((width, share), jnp.bfloat16),
        compiler_params=pltpu.CompilerParams(vmem_limit_bytes=VMEM_BYTES // 2),
        cost_estimate=pl.CostEstimate(
            flops=2 * rows * width * share,
            bytes_accessed=2 * (rows * (width + share) + width * share),
            transcendentals=0,
        ),
    )(*lefts, *rights)


def outer(left, right):
    return lax.dot_general(
        left, right, (((0,), (0,)), ((), ())), preferred_element_type=jnp.float32
    ).astype(jnp.bfloat16)


def local(tokens, d_out, row_expert, w_gate_up, w_down):
    row_count, feature_share = tokens.shape
    hidden_width = w_down.shape[1]
    expert_count = lax.axis_size("exp")
    gate_up_matrix = w_gate_up.reshape(feature_share, 2 * hidden_width)
    down_matrix = w_down.reshape(hidden_width, feature_share)
    cap = 2 * row_count // expert_count
    bounds = (0, cap // 2, cap)

    rank = rank_in_expert(row_expert)
    is_spill = rank >= cap
    busiest = jnp.max(jnp.where(is_spill, row_expert, -1))
    is_busiest = lax.axis_index("exp") == busiest
    spill_hot = one_hot(jnp.where(is_spill, rank - cap, -1), cap)
    chunk_hot = []
    for low, high in zip(bounds, bounds[1:]):
        inside = (rank >= low) & (rank < high)
        slot = row_expert * (high - low) + rank - low
        chunk_hot.append(one_hot(jnp.where(inside, slot, -1), expert_count * (high - low)))

    both = jnp.concatenate([tokens, d_out], axis=1)

    def split(both_in):
        return both_in[:, :feature_share], both_in[:, feature_share:]

    def products(rows_in, rows_block, grads_in, grads_block):
        parts = product(rows_in, rows_block, feature_share, gate_up_matrix, False, 2)
        parts += product(grads_in, grads_block, feature_share, down_matrix, True, 1)
        return [pair_over_grp(part) for part in parts]

    always = jnp.ones((1,), jnp.int32)
    only_busiest = is_busiest.astype(jnp.int32).reshape(1)

    far = outer_masks()
    spill_both = place(spill_hot, both)
    for mask in far:
        spill_both = double(spill_both, mask)
    spill_rows, spill_grads = split(spill_both)
    sent_0 = place(chunk_hot[0], both)
    spill_rows, spill_grads, sent_0 = lax.optimization_barrier((spill_rows, spill_grads, sent_0))

    arrived_0 = exchange(sent_0, expert_count)
    spill_rows = double(double(spill_rows, 2), 1)
    spill_grads = swap_quarters(double(double(spill_grads, 1), 2))
    sent_1 = place(chunk_hot[1], both)
    arrived_0, spill_rows, spill_grads, sent_1, gate_up_matrix = lax.optimization_barrier(
        (arrived_0, spill_rows, spill_grads, sent_1, gate_up_matrix)
    )

    arrived_1 = exchange(sent_1, expert_count)
    out_s, hidden_s, branch_s = finish(
        only_busiest, *products(spill_rows, 0, spill_grads, 0), gate_up_matrix
    )
    middle = feature_share // 2
    kept_a, sent_a = halves(out_s[:, :middle])
    kept_b, sent_b = halves(swap_quarters(out_s[:, middle:]))
    arrived_0, kept_a, sent_a, kept_b, sent_b = lax.optimization_barrier(
        (arrived_0, kept_a, sent_a, kept_b, sent_b)
    )
    come_a, come_b = swap_with(sent_a, 1), swap_with(sent_b, 2)
    out_0, hidden_0, branch_0 = finish(
        always, *products(arrived_0, 0, arrived_0, 1), gate_up_matrix
    )
    rows_0, _ = split(arrived_0)
    arrived_1, out_0, come_a, come_b, rows_0 = lax.optimization_barrier(
        (arrived_1, out_0, come_a, come_b, rows_0)
    )

    back_0 = exchange(out_0, expert_count)
    kept_a, sent_a = halves(kept_a + come_a)
    kept_b, sent_b = halves(kept_b + come_b)
    come_a, come_b = swap_with(sent_a, 2), swap_with(sent_b, 1)
    out_1, hidden_1, branch_1 = finish(
        always, *products(arrived_1, 0, arrived_1, 1), gate_up_matrix
    )
    back_0, come_a, come_b, out_1, arrived_1 = lax.optimization_barrier(
        (back_0, come_a, come_b, out_1, arrived_1)
    )
    back_s = jnp.concatenate([kept_a + come_a, kept_b + come_b], axis=1)

    for mask in reversed(far[1:]):
        back_s = halve(back_s, mask)
    rows_1, _ = split(arrived_1)
    back_1 = exchange(out_1, expert_count)

    all_rows = jnp.concatenate([spill_rows, rows_0, rows_1], axis=0)
    branch = jnp.concatenate([branch_s, branch_0, branch_1], axis=0)
    gate_up_grads = with_layout_constraint(outer(all_rows, branch), Layout((0, 1)))
    down_grads = outer_of_pieces(
        (hidden_s, hidden_0, hidden_1),
        (spill_grads, arrived_0, arrived_1),
        (0, 1, 1),
        feature_share,
    ).reshape(1, hidden_width, feature_share)
    gate_up_grads = gate_up_grads.reshape(feature_share // 8, 8, 2, hidden_width)
    back_s, gate_up_grads, down_grads = lax.optimization_barrier(
        (back_s, gate_up_grads.transpose(0, 2, 1, 3), down_grads)
    )

    back_s = halve(back_s, far[0])
    gate_up_grads = gate_up_grads.transpose(0, 2, 1, 3).reshape(
        1, feature_share, 2, hidden_width
    )

    pick = jnp.concatenate([spill_hot] + chunk_hot, axis=0)
    returned = jnp.concatenate([back_s, back_0, back_1], axis=0)
    token_grads = lax.dot_general(
        pick, returned, (((0,), (0,)), ((), ())), preferred_element_type=jnp.float32
    ).astype(jnp.bfloat16)
    return (token_grads, gate_up_grads, down_grads)


def solution(mesh):
    return jax.shard_map(
        local,
        mesh=mesh,
        in_specs=(
            P("exp", "grp"),
            P("exp", "grp"),
            P("exp"),
            P("exp", "grp", None, None),
            P("exp", None, "grp"),
        ),
        out_specs=(P("exp", "grp"), P("exp", "grp", None, None), P("exp", None, "grp")),
        check_vma=False,
    )
```

```python
import functools

import jax
import jax.numpy as jnp
from jax import lax
from jax.experimental import pallas as pl
from jax.experimental.layout import Layout, with_layout_constraint
from jax.experimental.pallas import tpu as pltpu
from jax.sharding import PartitionSpec as P

VMEM_BYTES = 48 * 1024 * 1024
SMALL_COST = pl.CostEstimate(flops=1, bytes_accessed=1, transcendentals=0)


def rank_in_expert(row_expert):
    row_count = row_expert.shape[0]
    same = row_expert[:, None] == row_expert[None, :]
    earlier = jnp.arange(row_count)[None, :] < jnp.arange(row_count)[:, None]
    return jnp.sum((same & earlier).astype(jnp.int32), axis=1)


def one_hot(index, total):
    return (index[None, :] == jnp.arange(total, dtype=jnp.int32)[:, None]).astype(jnp.bfloat16)


def place(one_hot_rows, rows):
    return lax.dot_general(
        one_hot_rows, rows, (((1,), (0,)), ((), ())), preferred_element_type=jnp.float32
    ).astype(jnp.bfloat16)


def exchange(rows, expert_count):
    slots, width = rows.shape
    return lax.all_to_all(
        rows.reshape(expert_count, slots // expert_count, width),
        "exp",
        split_axis=0,
        concat_axis=0,
        tiled=True,
    ).reshape(slots, width)


def swap_with(rows, mask):
    total = lax.axis_size("exp")
    return lax.ppermute(rows, "exp", [(i, i ^ mask) for i in range(total)])


def double(rows, mask):
    return jnp.concatenate([rows, swap_with(rows, mask)], axis=0)


def halves(rows):
    half = rows.shape[0] // 2
    return rows[:half], rows[half:]


def halve(rows, mask):
    kept, sent = halves(rows)
    return kept + swap_with(sent, mask)


def outer_masks():
    masks = []
    bit = lax.axis_size("exp") // 2
    while bit > 2:
        masks.append(bit)
        bit //= 2
    return masks


def swap_quarters(rows):
    quarter = rows.shape[0] // 4
    parts = [rows[i * quarter : (i + 1) * quarter] for i in (0, 2, 1, 3)]
    return jnp.concatenate(parts, axis=0)


def block_of(extent, most):
    size = most
    while extent % size:
        size //= 2
    return size


def dot_f32(left, right, left_dim, right_dim):
    return lax.dot_general(
        left, right, (((left_dim,), (right_dim,)), ((), ())), preferred_element_type=jnp.float32
    )


def product_kernel(right_dim, steps, left_ref, right_ref, *out_refs):
    for piece, out_ref in enumerate(out_refs):

        @pl.when(pl.program_id(0) // steps == piece)
        def _():
            out_ref[...] = dot_f32(left_ref[...], right_ref[...], 1, right_dim).astype(
                out_ref.dtype
            )


def product(left, column_block, depth, right, transposed, pieces):
    height = left.shape[0]
    width = right.shape[0] if transposed else right.shape[1]
    share = width // pieces
    step = block_of(share, 256)
    steps = share // step
    if transposed:
        right_spec = pl.BlockSpec((step, depth), lambda j: (j, 0))
    else:
        right_spec = pl.BlockSpec((depth, step), lambda j: (0, j))

    def place_of(piece):
        return lambda j: (0, jnp.clip(j - piece * steps, 0, steps - 1))

    return pl.pallas_call(
        functools.partial(product_kernel, 1 if transposed else 0, steps),
        grid=(width // step,),
        in_specs=[pl.BlockSpec((height, depth), lambda j: (0, column_block)), right_spec],
        out_specs=[pl.BlockSpec((height, step), place_of(piece)) for piece in range(pieces)],
        out_shape=[jax.ShapeDtypeStruct((height, share), jnp.bfloat16)] * pieces,
        compiler_params=pltpu.CompilerParams(vmem_limit_bytes=VMEM_BYTES),
        cost_estimate=SMALL_COST,
    )(left, right)


def pair_over_grp(part):
    if lax.axis_size("grp") == 2:
        return part, lax.ppermute(part, "grp", [(0, 1), (1, 0)])
    return lax.psum(part, "grp"), jnp.zeros_like(part)


def finish_kernel(pieces, keep_ref, *refs):
    pairs = [(refs[2 * i], refs[2 * i + 1]) for i in range(3 * pieces)]
    matrix_ref, out_ref, hidden_ref, branch_ref = refs[6 * pieces :]
    height, width = hidden_ref.shape
    share = width // pieces

    @pl.when(pl.program_id(0) == 0)
    def _():
        keep = keep_ref[0] > 0
        step = block_of(height, 32)

        @pl.loop(0, height // step)
        def _(i):
            here = pl.ds(pl.multiple_of(i * step, step), step)

            def total(pair):
                one, two = pair
                return one[here, :].astype(jnp.float32) + two[here, :].astype(jnp.float32)

            def put(ref, first, value):
                kept = jnp.where(keep, value, 0.0).astype(ref.dtype)
                ref[here, pl.ds(first, share)] = kept

            for piece in range(pieces):
                gate_value = total(pairs[piece])
                upward = total(pairs[pieces + piece])
                hidden_grads = total(pairs[2 * pieces + piece])
                sigmoid_value = jax.nn.sigmoid(gate_value)
                activated = gate_value * sigmoid_value
                gate_slope = sigmoid_value * (1.0 + gate_value * (1.0 - sigmoid_value))
                first = piece * share
                put(hidden_ref, first, activated * upward)
                put(branch_ref, first, hidden_grads * upward * gate_slope)
                put(branch_ref, width + first, hidden_grads * activated)

    out_ref[...] = dot_f32(branch_ref[...], matrix_ref[...], 1, 1).astype(out_ref.dtype)


def finish(keep, pairs, matrix):
    pieces = len(pairs) // 3
    height, share = pairs[0][0].shape
    width = pieces * share
    features = matrix.shape[0]
    step = block_of(features, 512)
    whole = lambda columns: pl.BlockSpec((height, columns), lambda j: (0, 0))
    shape = lambda columns: jax.ShapeDtypeStruct((height, columns), jnp.bfloat16)
    return pl.pallas_call(
        functools.partial(finish_kernel, pieces),
        grid=(features // step,),
        in_specs=[
            pl.BlockSpec(memory_space=pltpu.SMEM),
        ]
        + [whole(share)] * (6 * pieces)
        + [
            pl.BlockSpec((step, 2 * width), lambda j: (j, 0)),
        ],
        out_specs=[
            pl.BlockSpec((height, step), lambda j: (0, j)),
            whole(width),
            whole(2 * width),
        ],
        out_shape=[shape(features), shape(width), shape(2 * width)],
        compiler_params=pltpu.CompilerParams(vmem_limit_bytes=VMEM_BYTES),
        cost_estimate=SMALL_COST,
    )(keep, *[part for pair in pairs for part in pair], matrix)


def outer_kernel(count, *refs):
    out_ref = refs[-1]
    total = dot_f32(refs[0][...], refs[count][...], 0, 0)
    for left_ref, right_ref in zip(refs[1:count], refs[count + 1 : -1]):
        total += dot_f32(left_ref[...], right_ref[...], 0, 0)
    out_ref[...] = total.astype(out_ref.dtype)


def outer_of_pieces(lefts, rights, shares, share):
    width = lefts[0].shape[1]
    step = block_of(share, 512)
    steps = share // step
    rows = sum(left.shape[0] for left in lefts)

    def columns(part):
        return lambda j: (0, part * steps + j)

    return pl.pallas_call(
        functools.partial(outer_kernel, len(lefts)),
        grid=(steps,),
        in_specs=[pl.BlockSpec(left.shape, lambda j: (0, 0)) for left in lefts]
        + [
            pl.BlockSpec((right.shape[0], step), columns(part))
            for right, part in zip(rights, shares)
        ],
        out_specs=pl.BlockSpec((width, step), lambda j: (0, j)),
        out_shape=jax.ShapeDtypeStruct((width, share), jnp.bfloat16),
        compiler_params=pltpu.CompilerParams(vmem_limit_bytes=VMEM_BYTES // 2),
        cost_estimate=pl.CostEstimate(
            flops=2 * rows * width * share,
            bytes_accessed=2 * (rows * (width + share) + width * share),
            transcendentals=0,
        ),
    )(*lefts, *rights)


def outer(left, right):
    return lax.dot_general(
        left, right, (((0,), (0,)), ((), ())), preferred_element_type=jnp.float32
    ).astype(jnp.bfloat16)


def local(tokens, d_out, row_expert, w_gate_up, w_down):
    row_count, feature_share = tokens.shape
    hidden_width = w_down.shape[1]
    expert_count = lax.axis_size("exp")
    gate_up_matrix = w_gate_up.reshape(feature_share, 2 * hidden_width)
    down_matrix = w_down.reshape(hidden_width, feature_share)
    cap = 2 * row_count // expert_count
    bounds = (0, cap // 2, cap)

    rank = rank_in_expert(row_expert)
    is_spill = rank >= cap
    busiest = jnp.max(jnp.where(is_spill, row_expert, -1))
    is_busiest = lax.axis_index("exp") == busiest
    spill_hot = one_hot(jnp.where(is_spill, rank - cap, -1), cap)
    chunk_hot = []
    for low, high in zip(bounds, bounds[1:]):
        inside = (rank >= low) & (rank < high)
        slot = row_expert * (high - low) + rank - low
        chunk_hot.append(one_hot(jnp.where(inside, slot, -1), expert_count * (high - low)))

    both = jnp.concatenate([tokens, d_out], axis=1)

    def split(both_in):
        return both_in[:, :feature_share], both_in[:, feature_share:]

    def products(rows_in, rows_block, grads_in, grads_block, pieces):
        parts = product(rows_in, rows_block, feature_share, gate_up_matrix, False, 2 * pieces)
        parts += product(grads_in, grads_block, feature_share, down_matrix, True, pieces)
        return [pair_over_grp(part) for part in parts]

    always = jnp.ones((1,), jnp.int32)
    only_busiest = is_busiest.astype(jnp.int32).reshape(1)

    far = outer_masks()
    spill_both = place(spill_hot, both)
    for mask in far:
        spill_both = double(spill_both, mask)
    spill_rows, spill_grads = split(spill_both)
    sent_0 = place(chunk_hot[0], both)
    spill_rows, spill_grads, sent_0 = lax.optimization_barrier((spill_rows, spill_grads, sent_0))

    arrived_0 = exchange(sent_0, expert_count)
    spill_rows = double(double(spill_rows, 2), 1)
    spill_grads = swap_quarters(double(double(spill_grads, 1), 2))
    sent_1 = place(chunk_hot[1], both)
    arrived_0, spill_rows, spill_grads, sent_1, gate_up_matrix = lax.optimization_barrier(
        (arrived_0, spill_rows, spill_grads, sent_1, gate_up_matrix)
    )

    arrived_1 = exchange(sent_1, expert_count)
    out_s, hidden_s, branch_s = finish(
        only_busiest, products(spill_rows, 0, spill_grads, 0, 1), gate_up_matrix
    )
    middle = feature_share // 2
    kept_a, sent_a = halves(out_s[:, :middle])
    kept_b, sent_b = halves(swap_quarters(out_s[:, middle:]))
    arrived_0, kept_a, sent_a, kept_b, sent_b = lax.optimization_barrier(
        (arrived_0, kept_a, sent_a, kept_b, sent_b)
    )
    come_a, come_b = swap_with(sent_a, 1), swap_with(sent_b, 2)
    out_0, hidden_0, branch_0 = finish(
        always, products(arrived_0, 0, arrived_0, 1, 1), gate_up_matrix
    )
    rows_0, _ = split(arrived_0)
    arrived_1, out_0, come_a, come_b, rows_0 = lax.optimization_barrier(
        (arrived_1, out_0, come_a, come_b, rows_0)
    )

    back_0 = exchange(out_0, expert_count)
    kept_a, sent_a = halves(kept_a + come_a)
    kept_b, sent_b = halves(kept_b + come_b)
    come_a, come_b = swap_with(sent_a, 2), swap_with(sent_b, 1)
    out_1, hidden_1, branch_1 = finish(
        always, products(arrived_1, 0, arrived_1, 1, 2), gate_up_matrix
    )
    back_0, come_a, come_b, out_1, arrived_1 = lax.optimization_barrier(
        (back_0, come_a, come_b, out_1, arrived_1)
    )
    back_s = jnp.concatenate([kept_a + come_a, kept_b + come_b], axis=1)

    for mask in reversed(far[1:]):
        back_s = halve(back_s, mask)
    rows_1, _ = split(arrived_1)
    back_1 = exchange(out_1, expert_count)

    all_rows = jnp.concatenate([spill_rows, rows_0, rows_1], axis=0)
    branch = jnp.concatenate([branch_s, branch_0, branch_1], axis=0)
    gate_up_grads = with_layout_constraint(outer(all_rows, branch), Layout((0, 1)))
    down_grads = outer_of_pieces(
        (hidden_s, hidden_0, hidden_1),
        (spill_grads, arrived_0, arrived_1),
        (0, 1, 1),
        feature_share,
    ).reshape(1, hidden_width, feature_share)
    gate_up_grads = gate_up_grads.reshape(feature_share // 8, 8, 2, hidden_width)
    back_s, gate_up_grads, down_grads = lax.optimization_barrier(
        (back_s, gate_up_grads.transpose(0, 2, 1, 3), down_grads)
    )

    back_s = halve(back_s, far[0])
    gate_up_grads = gate_up_grads.transpose(0, 2, 1, 3).reshape(
        1, feature_share, 2, hidden_width
    )

    pick = jnp.concatenate([spill_hot] + chunk_hot, axis=0)
    returned = jnp.concatenate([back_s, back_0, back_1], axis=0)
    token_grads = lax.dot_general(
        pick, returned, (((0,), (0,)), ((), ())), preferred_element_type=jnp.float32
    ).astype(jnp.bfloat16)
    return (token_grads, gate_up_grads, down_grads)


def solution(mesh):
    return jax.shard_map(
        local,
        mesh=mesh,
        in_specs=(
            P("exp", "grp"),
            P("exp", "grp"),
            P("exp"),
            P("exp", "grp", None, None),
            P("exp", None, "grp"),
        ),
        out_specs=(P("exp", "grp"), P("exp", "grp", None, None), P("exp", None, "grp")),
        check_vma=False,
    )
```
